256 devices in a mesh: seg: 16 (over y, x_lo, core), samp: 2 (over x_hi), dp: 8 (over z).
Axes of the slice: x: 4 (x_hi: 2, x_lo: 2; x = x_hi * 2 + x_lo), y: 4, z: 8, core: 2. Of those that a mesh axis runs over, the one named last changes fastest.
Arguments:
- head_start: bfloat16 [16384, 8192], P('dp', ('seg', 'samp')), may hold values from -6 to 6
- flow_start: bfloat16 [16384, 8192], P('dp', ('seg', 'samp')), may hold values from -4 to 4
- impedance: float32 [16384, 8], P('dp'), may hold values from 0.5 to 2
- friction: float32 [16384, 8], P('dp'), may hold values from 0.05 to 0.5
- seg_count: int32 [16384], P('dp'), may hold values from 1 to 8
- junction_code: int32 [16384, 8], P('dp'), may hold values from 0 to 2
- boundary_code: int32 [16384], P('dp'), may hold values from 0 to 2
- head_up: float32 [16384], P('dp'), may hold values from 0.5 to 2
- head_down: float32 [16384], P('dp'), may hold values from -1 to 1
- opening: float32 [16384], P('dp'), may hold values from 0.2 to 2
- window_start: int32 [16384], P('dp'), may hold values from 0 to 4096
- layer_weights: bfloat16 [2, 1024, 1024], replicated, may hold values from -0.1875 to 0.1875
Outputs:
- head_end: bfloat16 [16384, 8192], P('dp', ('seg', 'samp'))
- weight_grads: float32 [2, 1024, 1024], P(None, ('seg', 'samp', 'dp'))
The draws below stay inside these ranges and needn't reach their ends.
Inputs may be any that keep to these rules, and one draw needn't show every extreme that they name: Each pipe is cut into seg_count equal sections. `boundary_code`: 0 reservoir, 1 closed end, 2 valve.
All inputs are finite; a program needn't handle non-finite values.
Results may differ from the reference program's by a relative error of at most 0.0004.
The reference program's roundings to bfloat16 on the way count: a program that leaves them out, or rounds other values in their place, can miss the bound.
Values may be sent and summed in bfloat16 or wider, within the bound.
A program may use at most 128 MiB of HBM per device.

```python
import math
import jax
import jax.numpy as jnp
from jax import lax

HID = 1024
LAYERS = 2
MAXSEG = 8
DES_DEV = 2048
CELLS = 8192
DESIGNS = 16384
WIN = 4096
ROWS = 65536
N_DP = 8


def plant(drawn, rng, smallest, top_value):
    index_at = [jax.random.randint(jax.random.fold_in(rng, axis), (), 0, length) for axis, length in enumerate(drawn.shape)]
    main_axis = drawn.shape.index(max(drawn.shape))
    next_to = index_at[:main_axis] + [(index_at[main_axis] + 1) % drawn.shape[main_axis]] + index_at[main_axis + 1:]
    return drawn.at[tuple(index_at)].set(smallest).at[tuple(next_to)].set(top_value)


def block_scale(rng, shape, cuts, low, largest):
    def one(axis_at, blocks):
        heights = jax.random.uniform(jax.random.fold_in(jax.random.fold_in(rng, 6), axis_at), (blocks,), jnp.float32, low / len(cuts), largest / len(cuts))
        return jnp.repeat(jnp.exp(heights), shape[axis_at] // blocks).reshape((-1,) + (1,) * (len(shape) - axis_at - 1))

    gain = one(*cuts[0])
    for cut in cuts[1:]:
        gain = gain * one(*cut)
    return gain


def normal_values(key, dims, width, limit, shards=(), kind=jnp.bfloat16):
    values = jax.random.normal(key, dims, jnp.float32) * width
    if len(shards) > 0:
        values = block_scale(key, dims, shards, -0.22, 0.18) * values
    return jnp.clip(values, min=-limit, max=limit).astype(kind)


def setup_inputs(seed: int = 0) -> dict:
    key_of = jax.random.split(jax.random.key(seed), 13)
    head_start = normal_values(key_of[0], (DESIGNS, CELLS), 1.0, 6.0, ((0, 8), (1, 32)))
    flow_start = normal_values(key_of[1], (DESIGNS, CELLS), 0.5, 4.0, ((0, 8), (1, 32)))
    impedance = jnp.clip(jnp.exp(math.log(2.0) - 1.3862944 * jax.random.uniform(key_of[2], (DESIGNS, MAXSEG), jnp.float32) ** block_scale(key_of[2], (DESIGNS, MAXSEG), ((0, 8),), -0.2, 0.2)), 0.5, 2.0)
    friction = jnp.clip(jnp.exp(math.log(0.5) - 2.3025851 * jax.random.uniform(key_of[3], (DESIGNS, MAXSEG), jnp.float32) ** block_scale(key_of[3], (DESIGNS, MAXSEG), ((0, 8),), -0.2, 0.2)), 0.05, 0.5)
    seg_count = plant(jax.random.randint(key_of[4], (DESIGNS,), 1, MAXSEG + 1), jax.random.fold_in(key_of[4], 1), 1, MAXSEG).astype(jnp.int32)
    junction_code = plant(jax.random.randint(key_of[5], (DESIGNS, MAXSEG), 0, 3), jax.random.fold_in(key_of[5], 1), 0, 2).astype(jnp.int32)
    boundary_code = plant(jax.random.randint(key_of[6], (DESIGNS,), 0, 3), jax.random.fold_in(key_of[6], 1), 0, 2).astype(jnp.int32)
    head_up = jnp.clip(0.5 + 1.5 * jax.random.uniform(key_of[7], (DESIGNS,), jnp.float32) ** block_scale(key_of[7], (DESIGNS,), ((0, 8),), -0.2, 0.2), 0.5, 2.0)
    head_down = jnp.clip(jax.random.uniform(key_of[8], (DESIGNS,), jnp.float32, -1.0, 1.0) * block_scale(key_of[8], (DESIGNS,), ((0, 8),), -0.4, 0.0), -1.0, 1.0)
    opening = jnp.clip(jnp.exp(math.log(2.0) - 2.3025851 * jax.random.uniform(key_of[9], (DESIGNS,), jnp.float32) ** block_scale(key_of[9], (DESIGNS,), ((0, 8),), -0.2, 0.2)), 0.2, 2.0)
    window_start = plant(jax.random.randint(key_of[10], (DESIGNS,), 0, CELLS - WIN + 1), jax.random.fold_in(key_of[10], 1), 0, CELLS - WIN).astype(jnp.int32)
    layer_weights = normal_values(key_of[11], (LAYERS, HID, HID), HID ** -0.5, 0.1875)
    return {"head_start": head_start, "flow_start": flow_start, "impedance": impedance, "friction": friction, "seg_count": seg_count, "junction_code": junction_code, "boundary_code": boundary_code, "head_up": head_up, "head_down": head_down, "opening": opening, "window_start": window_start, "layer_weights": layer_weights}


def section_fields(glob_cells, seg_total, impedance, friction, junction, cell_total):
    placed = jnp.clip(glob_cells, 0, cell_total - 1)
    section = (placed[None, :] * seg_total[:, None]) // cell_total
    wave = jnp.zeros(section.shape, jnp.float32)
    damping = jnp.zeros(section.shape, jnp.float32)
    for section_id in range(impedance.shape[1]):
        picked = section == section_id
        wave = jnp.where(picked, impedance[:, section_id:section_id + 1], wave)
        damping = jnp.where(picked, friction[:, section_id:section_id + 1] * (1.0 + junction[:, section_id:section_id + 1].astype(jnp.float32)), damping)
    return wave, damping


def characteristic_step(heads, flows, wave, damping, glob_inner, params, cell_total):
    upper_head, lower_head, valve_open, boundary = params
    left_head = heads[:, :-2]
    left_flow = flows[:, :-2]
    right_head = heads[:, 2:]
    right_flow = flows[:, 2:]
    forward_char = left_head + wave * left_flow - damping * left_flow * jnp.abs(left_flow)
    backward_char = right_head - wave * right_flow + damping * right_flow * jnp.abs(right_flow)
    new_head = 0.5 * (forward_char + backward_char)
    new_flow = (forward_char - backward_char) / (2.0 * wave)
    at_start = (glob_inner == 0)[None, :]
    at_finish = (glob_inner == cell_total - 1)[None, :]
    valve_head = forward_char / (1.0 + wave * valve_open)
    end_head = jnp.where(boundary == 0, lower_head, jnp.where(boundary == 1, forward_char, valve_head))
    end_flow = jnp.where(boundary == 0, (forward_char - lower_head) / wave, jnp.where(boundary == 1, jnp.zeros_like(forward_char), valve_open * valve_head))
    new_head = jnp.where(at_start, upper_head, jnp.where(at_finish, end_head, new_head))
    new_flow = jnp.where(at_start, (upper_head - backward_char) / wave, jnp.where(at_finish, end_flow, new_flow))
    return new_head, new_flow


def operator_grads(inputs, targets, layer_weights, row_total):
    layers = layer_weights.shape[0]
    activations = [inputs]
    pre_values = []
    current = inputs
    output = None
    for layer_number in range(layers):
        product = jnp.dot(current, layer_weights[layer_number], preferred_element_type=jnp.float32)
        if layer_number + 1 < layers:
            pre_values.append(product)
            current = jax.nn.silu(product).astype(jnp.bfloat16)
            activations.append(current)
        else:
            output = product
    error = output - targets.astype(jnp.float32)
    grad_rows = (error * (8.0 / row_total)).astype(jnp.bfloat16)
    grads = [None] * layers
    for layer_number in reversed(range(layers)):
        grads[layer_number] = jnp.dot(activations[layer_number].T, grad_rows, preferred_element_type=jnp.float32)
        if layer_number > 0:
            back = jnp.dot(grad_rows, layer_weights[layer_number].T, preferred_element_type=jnp.float32)
            pre_value = pre_values[layer_number - 1]
            sigma = jax.nn.sigmoid(pre_value)
            grad_rows = (back * sigma * (1.0 + pre_value * (1.0 - sigma))).astype(jnp.bfloat16)
    return jnp.stack(grads)


def reference(head_start, flow_start, impedance, friction, seg_count, junction_code, boundary_code, head_up, head_down, opening, window_start, layer_weights):
    glob_inner = jnp.arange(CELLS, dtype=jnp.int32)

    def one_block(block):
        heads_in, flows_in, imped, fric, counts, junction, boundary, upper, lower, valve = block
        wave, damping = section_fields(glob_inner, counts, imped, fric, junction, CELLS)
        params = (upper[:, None], lower[:, None], valve[:, None], boundary[:, None])
        heads = heads_in.astype(jnp.float32)
        flows = flows_in.astype(jnp.float32)
        for step_number in range(2):
            heads, flows = characteristic_step(jnp.pad(heads, ((0, 0), (1, 1))), jnp.pad(flows, ((0, 0), (1, 1))), wave, damping, glob_inner, params, CELLS)
        return heads.astype(jnp.bfloat16)

    def split(array):
        return array.reshape((N_DP, DES_DEV) + array.shape[1:])

    blocks = tuple(split(item) for item in (head_start, flow_start, impedance, friction, seg_count, junction_code, boundary_code, head_up, head_down, opening))
    head_end = lax.map(one_block, blocks).reshape(DESIGNS, CELLS)
    cutter = jax.vmap(lambda row_values, begin: lax.dynamic_slice_in_dim(row_values, begin, WIN))
    inputs = cutter(head_start, window_start.astype(jnp.int32)).reshape(ROWS, HID)
    targets = cutter(head_end, window_start.astype(jnp.int32)).reshape(ROWS, HID)
    weight_grads = operator_grads(inputs, targets, layer_weights, ROWS)
    return head_end, weight_grads
```

```python
import functools
import jax
import jax.numpy as jnp
from jax import lax
from jax.experimental import pallas as pl
from jax.experimental.pallas import tpu as pltpu
from jax.sharding import PartitionSpec as P

MESH = pl.DeviceIdType.MESH
GROUP = ("seg", "samp")
PLANE = 32
CELLS = 8192
BF16 = jnp.bfloat16
F32 = jnp.float32


def dot(lhs, rhs, lhs_dim, rhs_dim):
    return lax.dot_general(
        lhs, rhs, (((lhs_dim,), (rhs_dim,)), ((), ())), preferred_element_type=F32
    )


def pack_kernel(head_ref, flow_ref, out_ref):
    row = lax.broadcasted_iota(jnp.int32, (16, 256), 0)
    lane = lax.broadcasted_iota(jnp.int32, (16, 256), 1)
    wanted = jnp.where(row < 2, row, row + 252)
    pick = jnp.where((row < 4) & (lane == wanted), 1.0, 0.0).astype(BF16)
    heads = dot(pick, head_ref[...], 1, 1)
    flows = dot(pick, flow_ref[...], 1, 1)
    out_ref[0:2] = heads[0:2].astype(BF16)
    out_ref[2:4] = flows[0:2].astype(BF16)
    out_ref[4:6] = heads[2:4].astype(BF16)
    out_ref[6:8] = flows[2:4].astype(BF16)


def pack_edges(head, flow):
    return pl.pallas_call(
        pack_kernel, out_shape=jax.ShapeDtypeStruct((8, head.shape[0]), BF16)
    )(head, flow)


def stencil_kernel(table_ref, head_ref, flow_ref, halo_ref, out_ref, edge):
    rows = head_ref.shape[0]
    position = lax.axis_index(GROUP)
    first = position * 256
    row = lax.broadcasted_iota(jnp.int32, (8, 256), 0)
    lane2 = lax.broadcasted_iota(jnp.int32, (8, 256), 1)
    wanted = jnp.where(row < 4, (row % 2), 126 + (row % 2)) + jnp.where((row % 4) < 2, 0, 128)
    place = jnp.where(lane2 == wanted, 1.0, 0.0).astype(BF16)
    edge[...] = dot(halo_ref[...], place, 0, 0)
    step = 16
    lane = lax.broadcasted_iota(jnp.int32, (step, 384), 1)
    cell = jnp.where(lane < 320, lane, lane - 384) + first
    placed = jnp.clip(cell, 0, CELLS - 1)
    at_start = cell == 0
    at_finish = cell == CELLS - 1

    def run(is_edge, chunk, carry):
        here = pl.ds(pl.multiple_of(chunk * step, step), step)
        table = table_ref[here, :]
        count = table[:, 24:25].astype(jnp.int32)
        section = lax.shift_right_logical(placed * count, 13)

        def look(base):
            return jnp.concatenate(
                [
                    jnp.take_along_axis(table, section[:, c * 128 : c * 128 + 128] + base, axis=1)
                    for c in range(3)
                ],
                axis=1,
            )

        wave = look(0)
        loss = look(8)
        half = look(16)
        ends = edge[here, :]
        heads = jnp.concatenate([head_ref[here, :].astype(F32), ends[:, :128]], axis=1)
        flows = jnp.concatenate([flow_ref[here, :].astype(F32), ends[:, 128:]], axis=1)
        upper = table[:, 25:26]
        lower = table[:, 26:27]
        valve = table[:, 27:28]
        kind = table[:, 28:29]
        for number in range(2):
            lh = pltpu.roll(heads, 1, 1)
            lq = pltpu.roll(flows, 1, 1)
            rh = pltpu.roll(heads, 383, 1)
            rq = pltpu.roll(flows, 383, 1)
            if number == 1:
                lh, lq, rh, rq = (v[:, :256] for v in (lh, lq, rh, rq))
                wave, loss, half = (v[:, :256] for v in (wave, loss, half))
            forward = lh + wave * lq - loss * lq * jnp.abs(lq)
            backward = rh - wave * rq + loss * rq * jnp.abs(rq)
            width = forward.shape[1]
            new_heads = 0.5 * (forward + backward)
            if number == 0:
                new_flows = (forward - backward) * half
            if is_edge:
                start, finish = at_start[:, :width], at_finish[:, :width]
                valve_head = forward / (1.0 + wave * valve)
                end_head = jnp.where(kind == 0.0, lower, jnp.where(kind == 1.0, forward, valve_head))
                new_heads = jnp.where(start, upper, jnp.where(finish, end_head, new_heads))
                if number == 0:
                    end_flow = jnp.where(
                        kind == 0.0,
                        (forward - lower) * (2.0 * half),
                        jnp.where(kind == 1.0, 0.0, valve * valve_head),
                    )
                    new_flows = jnp.where(
                        start,
                        (upper - backward) * (2.0 * half),
                        jnp.where(finish, end_flow, new_flows),
                    )
            if number == 0:
                heads, flows = new_heads, new_flows
        out_ref[here, :] = new_heads.astype(BF16)
        return carry

    inner = (position > 0) & (position < PLANE - 1)

    @pl.when(inner)
    def _():
        lax.fori_loop(0, rows // step, functools.partial(run, False), 0, unroll=2)

    @pl.when(jnp.logical_not(inner))
    def _():
        lax.fori_loop(0, rows // step, functools.partial(run, True), 0)


def stencil(table, head, flow, halo):
    total = head.shape[0]
    rows = 256
    return pl.pallas_call(
        stencil_kernel,
        grid=(total // rows,),
        in_specs=[
            pl.BlockSpec((rows, 128), lambda i: (i, 0)),
            pl.BlockSpec((rows, 256), lambda i: (i, 0)),
            pl.BlockSpec((rows, 256), lambda i: (i, 0)),
            pl.BlockSpec((8, rows), lambda i: (0, i)),
        ],
        out_specs=pl.BlockSpec((rows, 256), lambda i: (i, 0)),
        out_shape=jax.ShapeDtypeStruct(head.shape, BF16),
        scratch_shapes=[pltpu.VMEM((rows, 256), F32)],
        cost_estimate=pl.CostEstimate(
            flops=total * 256 * 60, bytes_accessed=4 << 20, transcendentals=0
        ),
    )(table, head, flow, halo)


def cut_windows(rows_ref, begin_ref, out_ref):
    def group(number, carry):
        here = pl.ds(pl.multiple_of(number * 16, 16), 16)
        begin = begin_ref[here, :]
        block = lax.shift_right_logical(begin, 7)
        rest = begin & 127
        lane = lax.broadcasted_iota(jnp.int32, (16, 128), 1)
        values = []
        for source in range(PLANE):
            pair = rows_ref[source, here, :].astype(F32)
            values += [pair[:, :128], pair[:, 128:]]
        for bit, count in ((32, 64), (16, 48), (8, 40), (4, 36), (2, 34), (1, 33)):
            on = (block & bit) != 0
            values = [
                jnp.where(on, values[j + bit], values[j]) if j + bit < len(values) else values[j]
                for j in range(count)
            ]
        index = (lane + rest) & 127
        keep = lane + rest < 128
        turned = [jnp.take_along_axis(v, index, axis=1) for v in values]
        for j in range(32):
            piece = jnp.where(keep, turned[j], turned[j + 1]).astype(BF16)
            at = pl.ds(pl.multiple_of((j // 8) * 64 + number * 16, 16), 16)
            out_ref[at, (j % 8) * 128 : (j % 8) * 128 + 128] = piece
        return carry

    lax.fori_loop(0, 4, group, 0)


def forward_kernel(rows_ref, begin_ref, weights_ref, a0_ref, a1_ref, z_ref, out_ref):
    cut_windows(rows_ref, begin_ref, a0_ref)
    z = dot(a0_ref[...], weights_ref[0], 1, 0)
    z_ref[...] = z
    a1 = (z * jax.nn.sigmoid(z)).astype(BF16)
    a1_ref[...] = a1
    out_ref[...] = dot(a1, weights_ref[1], 1, 0)


def forward(rows, begin, weights):
    return pl.pallas_call(
        forward_kernel,
        out_shape=[
            jax.ShapeDtypeStruct((256, 1024), BF16),
            jax.ShapeDtypeStruct((256, 1024), BF16),
            jax.ShapeDtypeStruct((256, 1024), F32),
            jax.ShapeDtypeStruct((256, 1024), F32),
        ],
        compiler_params=pltpu.CompilerParams(vmem_limit_bytes=48 << 20),
        cost_estimate=pl.CostEstimate(
            flops=4 * 256 * 1024 * 1024, bytes_accessed=8 << 20, transcendentals=0
        ),
    )(rows, begin, weights)


def backward_kernel(scale, rows_ref, begin_ref, weights_ref, a0_ref, a1_ref, z_ref, output_ref, grads_ref, targets):
    cut_windows(rows_ref, begin_ref, targets)
    g1 = ((output_ref[...] - targets[...].astype(F32)) * scale).astype(BF16)
    grads_ref[1] = dot(a1_ref[...], g1, 0, 0)
    back = dot(g1, weights_ref[1], 1, 1)
    z = z_ref[...]
    sigma = jax.nn.sigmoid(z)
    g0 = (back * sigma * (1.0 + z * (1.0 - sigma))).astype(BF16)
    grads_ref[0] = dot(a0_ref[...], g0, 0, 0)


def backward(rows, begin, weights, a0, a1, z, output, scale):
    return pl.pallas_call(
        functools.partial(backward_kernel, scale),
        out_shape=jax.ShapeDtypeStruct((2, 1024, 1024), F32),
        scratch_shapes=[pltpu.VMEM((256, 1024), BF16)],
        compiler_params=pltpu.CompilerParams(vmem_limit_bytes=48 << 20),
        cost_estimate=pl.CostEstimate(
            flops=6 * 256 * 1024 * 1024, bytes_accessed=16 << 20, transcendentals=0
        ),
    )(rows, begin, weights, a0, a1, z, output)


def reduce_kernel(p_ref, out_ref, mine, other, a_in, b_in, a_sum, b_sum, a2_in, b2_in, z_sum, z_in, send, recv):
    seg, samp, z = lax.axis_index("seg"), lax.axis_index("samp"), lax.axis_index("dp")
    y, xlo, core = seg // 4, (seg // 2) % 2, seg % 2
    x = samp * 2 + xlo

    def at_x(t):
        return {"seg": y * 4 + (t % 2) * 2 + core, "samp": t // 2}

    def at_y(t):
        return {"seg": t * 4 + xlo * 2 + core}

    def at_z(t):
        return {"dp": t}

    at_core = {"seg": y * 4 + xlo * 2 + 1 - core}

    barrier = pltpu.get_barrier_semaphore()
    pl.semaphore_signal(barrier, inc=1, device_id=at_core, device_id_type=MESH)
    for p in range(1, 4):
        pl.semaphore_signal(barrier, inc=1, device_id=at_x((x + p) % 4), device_id_type=MESH)
        pl.semaphore_signal(barrier, inc=1, device_id=at_y((y + p) % 4), device_id_type=MESH)
    for p in range(1, 8):
        pl.semaphore_signal(barrier, inc=1, device_id=at_z((z + p) % 8), device_id_type=MESH)
    pl.semaphore_wait(barrier, 14)

    def copy(src, dst, number, device):
        return pltpu.make_async_remote_copy(
            src_ref=src,
            dst_ref=dst,
            send_sem=send.at[number],
            recv_sem=recv.at[number],
            device_id=device,
            device_id_type=MESH,
        )

    first = copy(p_ref.at[:, 1 - core], other, 0, at_core)
    first.start()
    first.wait()

    def add_core(i, c):
        mine[i] = p_ref[i, core] + other[i]
        return c

    lax.fori_loop(0, 16, add_core, 0)

    copies = []
    for p in range(1, 4):
        tx, ty = (x + p) % 4, (y + p) % 4
        for layer in range(2):
            for yy in range(4):
                k = 1 + ((p - 1) * 2 + layer) * 4 + yy
                copies.append(
                    copy(
                        mine.at[layer * 8 + yy * 2 + tx % 2, pl.ds(pl.multiple_of((tx // 2) * 32, 32), 32), pl.ds(0, 512)],
                        a_in.at[p - 1, layer * 4 + yy],
                        k,
                        at_x(tx),
                    )
                )
            for xx in range(2):
                k = 25 + ((p - 1) * 2 + layer) * 2 + xx
                copies.append(
                    copy(
                        mine.at[layer * 8 + ty * 2 + xx, :, pl.ds(512, 512)],
                        b_in.at[p - 1, layer * 2 + xx],
                        k,
                        at_y(ty),
                    )
                )
    for c in copies:
        c.start()
    for c in copies:
        c.wait()

    def add_a(i, c):
        own = mine[2 * i + xlo, pl.ds(pl.multiple_of(samp * 32, 32), 32), pl.ds(0, 512)]
        a_sum[i] = (own + a_in[0, i]) + (a_in[1, i] + a_in[2, i])
        return c

    lax.fori_loop(0, 8, add_a, 0)

    def add_b(i, c):
        own = mine[(i // 2) * 8 + y * 2 + i % 2, :, pl.ds(512, 512)]
        b_sum[i] = (own + b_in[0, i]) + (b_in[1, i] + b_in[2, i])
        return c

    lax.fori_loop(0, 4, add_b, 0)

    copies = []
    for p in range(1, 4):
        tx, ty = (x + p) % 4, (y + p) % 4
        for layer in range(2):
            k = 37 + (p - 1) * 2 + layer
            copies.append(copy(a_sum.at[layer * 4 + ty], a2_in.at[p - 1, layer], k, at_y(ty)))
            k = 43 + (p - 1) * 2 + layer
            copies.append(
                copy(
                    b_sum.at[layer * 2 + tx % 2, pl.ds(pl.multiple_of((tx // 2) * 32, 32), 32)],
                    b2_in.at[p - 1, layer],
                    k,
                    at_x(tx),
                )
            )
    for c in copies:
        c.start()
    for c in copies:
        c.wait()
    for layer in range(2):
        left = (a_sum[layer * 4 + y] + a2_in[0, layer]) + (a2_in[1, layer] + a2_in[2, layer])
        own = b_sum[layer * 2 + xlo, pl.ds(pl.multiple_of(samp * 32, 32), 32)]
        right = (own + b2_in[0, layer]) + (b2_in[1, layer] + b2_in[2, layer])
        for t in range(8):
            z_sum[t, 4 * layer : 4 * layer + 4, 0:512] = left[4 * t : 4 * t + 4]
            z_sum[t, 4 * layer : 4 * layer + 4, 512:1024] = right[4 * t : 4 * t + 4]
    copies = []
    for p in range(1, 8):
        t = (z + p) % 8
        copies.append(copy(z_sum.at[t], z_in.at[p - 1], 48 + p, at_z(t)))
    for c in copies:
        c.start()
    for c in copies:
        c.wait()
    total = z_sum[z]
    for p in range(7):
        total = total + z_in[p]
    out_ref[0] = total[0:4]
    out_ref[1] = total[4:8]


def reduce_scatter(grads):
    return pl.pallas_call(
        reduce_kernel,
        out_shape=jax.ShapeDtypeStruct((2, 4, 1024), F32),
        in_specs=[pl.BlockSpec(memory_space=pltpu.VMEM)],
        out_specs=pl.BlockSpec(memory_space=pltpu.VMEM),
        scratch_shapes=[
            pltpu.VMEM((16, 64, 1024), F32),
            pltpu.VMEM((16, 64, 1024), F32),
            pltpu.VMEM((3, 8, 32, 512), F32),
            pltpu.VMEM((3, 4, 64, 512), F32),
            pltpu.VMEM((8, 32, 512), F32),
            pltpu.VMEM((4, 64, 512), F32),
            pltpu.VMEM((3, 2, 32, 512), F32),
            pltpu.VMEM((3, 2, 32, 512), F32),
            pltpu.VMEM((8, 8, 1024), F32),
            pltpu.VMEM((7, 8, 1024), F32),
            pltpu.SemaphoreType.DMA((56,)),
            pltpu.SemaphoreType.DMA((56,)),
        ],
        compiler_params=pltpu.CompilerParams(
            collective_id=1, has_side_effects=True, vmem_limit_bytes=56 << 20
        ),
    )(grads.reshape(16, 2, 64, 1024))


def make_table(impedance, friction, seg_count, junction, boundary, head_up, head_down, opening):
    rows = impedance.shape[0]
    parts = [
        impedance,
        friction * (1.0 + junction.astype(F32)),
        0.5 / impedance,
        seg_count.astype(F32)[:, None],
        head_up[:, None],
        head_down[:, None],
        opening[:, None],
        boundary.astype(F32)[:, None],
        jnp.zeros((rows, 128 - 29), F32),
    ]
    return jnp.concatenate(parts, axis=1)


def spread(block):
    return lax.all_to_all(
        block.reshape(PLANE, 64, 256), GROUP, split_axis=0, concat_axis=0, tiled=True
    )


def body(
    head_start,
    flow_start,
    impedance,
    friction,
    seg_count,
    junction_code,
    boundary_code,
    head_up,
    head_down,
    opening,
    window_start,
    layer_weights,
):
    start_rows = spread(head_start)
    packed = pack_edges(head_start, flow_start)
    up = [(i, i + 1) for i in range(PLANE - 1)]
    down = [(i + 1, i) for i in range(PLANE - 1)]
    above = lax.ppermute(packed[:4], GROUP, down)
    below = lax.ppermute(packed[4:], GROUP, up)
    halo = jnp.concatenate([above, below], axis=0)
    table = make_table(
        impedance, friction, seg_count, junction_code, boundary_code, head_up, head_down, opening
    )
    head_end = stencil(table, head_start, flow_start, halo)
    end_rows = spread(head_end)
    begin = lax.dynamic_slice_in_dim(window_start, lax.axis_index(GROUP) * 64, 64)
    begin = jnp.broadcast_to(begin[:, None], (64, 128))
    a0, a1, z, output = forward(start_rows, begin, layer_weights)
    row_total = window_start.shape[0] * lax.axis_size("dp") * 4
    grads = backward(end_rows, begin, layer_weights, a0, a1, z, output, 8.0 / row_total)
    return (head_end, reduce_scatter(grads))


def solution(mesh):
    placed = (
        P("dp", ("seg", "samp")),
        P("dp", ("seg", "samp")),
        P("dp", None),
        P("dp", None),
        P("dp"),
        P("dp", None),
        P("dp"),
        P("dp"),
        P("dp"),
        P("dp"),
        P("dp"),
        P(),
    )
    return jax.shard_map(
        body,
        mesh=mesh,
        in_specs=placed,
        out_specs=(P("dp", ("seg", "samp")), P(None, ("seg", "samp", "dp"), None)),
        check_vma=False,
    )
```

```python
import functools
import jax
import jax.numpy as jnp
from jax import lax
from jax.experimental import pallas as pl
from jax.experimental.pallas import tpu as pltpu
from jax.sharding import PartitionSpec as P

MESH = pl.DeviceIdType.MESH
PLANE = 32
CELLS = 8192
BF16 = jnp.bfloat16
F32 = jnp.float32
I16 = jnp.int16
TOP = 32767.0


def dot(lhs, rhs, lhs_dim, rhs_dim):
    return lax.dot_general(
        lhs, rhs, (((lhs_dim,), (rhs_dim,)), ((), ())), preferred_element_type=F32
    )


def iota(shape, dim):
    return lax.broadcasted_iota(jnp.int32, shape, dim)


def eye(size):
    return jnp.where(iota((size, size), 0) == iota((size, size), 1), 1.0, 0.0).astype(BF16)


W_LO, W_HI, L_LO, L_HI, H_LO, H_HI, FIRST, COUNT, END_A, END_L, END_Q, UPPER = range(12)


def prepare_params(position, imp_ref, fric_ref, junc_ref, count_ref, kind_ref, up_ref, down_ref, open_ref, prm):
    wide = imp_ref.shape
    imp = imp_ref[...]
    loss = fric_ref[...] * (1.0 + junc_ref[...].astype(F32))
    count = count_ref[...]
    before = position * 256 - 1
    section = lax.shift_right_logical(jnp.maximum(before, 0) * count, 13)
    row = iota(wide, 0)

    def pick(values, number):
        return jnp.sum(jnp.where(row == number, values, 0.0), axis=0, keepdims=True)

    w_lo, w_hi = pick(imp, section), pick(imp, section + 1)
    w_end = pick(imp, count - 1)
    prm[W_LO : W_LO + 1] = w_lo
    prm[W_HI : W_HI + 1] = w_hi
    prm[L_LO : L_LO + 1] = pick(loss, section)
    prm[L_HI : L_HI + 1] = pick(loss, section + 1)
    prm[H_LO : H_LO + 1] = 0.5 / w_lo
    prm[H_HI : H_HI + 1] = 0.5 / jnp.where(w_hi == 0.0, 1.0, w_hi)
    prm[FIRST : FIRST + 1] = (before * count - (section + 1) * CELLS).astype(F32)
    prm[COUNT : COUNT + 1] = count.astype(F32)
    kind, valve = kind_ref[...], open_ref[...]
    factor = 1.0 / (1.0 + w_end * valve)
    prm[END_A : END_A + 1] = jnp.where(kind == 0, 0.0, jnp.where(kind == 1, 1.0, factor))
    prm[END_L : END_L + 1] = jnp.where(kind == 0, down_ref[...], 0.0)
    prm[END_Q : END_Q + 1] = jnp.where(kind == 0, 1.0 / w_end, jnp.where(kind == 1, 0.0, valve * factor))
    prm[UPPER : UPPER + 1] = up_ref[...]


def stencil_tile(position, tile, prm, heads, flows, h1, q1, turned):
    lanes = pl.ds(pl.multiple_of(tile * 128, 128), 128)

    def param(number, rows=8):
        return jnp.broadcast_to(prm[number : number + 1, lanes], (rows, 128))

    count = param(COUNT)
    start = param(FIRST) + iota((8, 128), 0).astype(F32) * count
    lows = [param(W_LO), param(L_LO), param(H_LO)]
    highs = [param(W_HI), param(L_HI), param(H_HI)]

    def fields(value, number):
        high = value >= 0.0
        return [jnp.where(high, highs[k], lows[k]) for k in range(number)]

    def ends(lh, lq, rh, rq, wave, loss):
        forward = lh + lq * (wave - loss * jnp.abs(lq))
        backward = rh - rq * (wave - loss * jnp.abs(rq))
        return forward, backward

    def first(g, value):
        wave, loss, half = fields(value, 3)
        left, right = pl.ds(8 * g + 6, 8), pl.ds(8 * g + 8, 8)
        forward, backward = ends(
            heads[tile, left, :], flows[tile, left, :], heads[tile, right, :], flows[tile, right, :], wave, loss
        )
        return forward, backward, half

    value = start
    for g in range(33):
        forward, backward, half = first(g, value)
        h1[8 * g : 8 * g + 8] = 0.5 * (forward + backward)
        q1[8 * g : 8 * g + 8] = (forward - backward) * half
        value = value + 8.0 * count

    @pl.when(position == 0)
    def _():
        _, backward, half = first(0, start)
        upper = param(UPPER)
        at = iota((8, 128), 0) == 1
        h1[0:8] = jnp.where(at, upper, h1[0:8])
        q1[0:8] = jnp.where(at, (upper - backward) * (2.0 * half), q1[0:8])

    @pl.when(position == PLANE - 1)
    def _():
        forward, _, _ = first(32, start + 256.0 * count)
        at = iota((8, 128), 0) == 0
        h1[256:264] = jnp.where(at, param(END_A) * forward + param(END_L), h1[256:264])
        q1[256:264] = jnp.where(at, (forward - param(END_L)) * param(END_Q), q1[256:264])

    def second(g, value):
        wave, loss = fields(value, 2)
        left, right = pl.ds(8 * g, 8), pl.ds(8 * g + 2, 8)
        return ends(h1[left, :], q1[left, :], h1[right, :], q1[right, :], wave, loss)

    value = start + count
    for g in range(16):
        pieces = []
        for _ in range(2):
            forward, backward = second(2 * g + len(pieces), value)
            pieces.append(0.5 * (forward + backward))
            value = value + 8.0 * count
        turned[16 * g : 16 * g + 16] = jnp.concatenate(pieces, axis=0).astype(BF16)

    @pl.when(position == 0)
    def _():
        at = iota((16, 128), 0) == 0
        turned[0:16] = jnp.where(at, param(UPPER, 16), turned[0:16].astype(F32)).astype(BF16)

    @pl.when(position == PLANE - 1)
    def _():
        forward, _ = second(31, start + 249.0 * count)
        last = param(END_A) * forward + param(END_L)
        last = jnp.concatenate([last, last], axis=0)
        at = iota((16, 128), 0) == 15
        turned[240:256] = jnp.where(at, last, turned[240:256].astype(F32)).astype(BF16)


def cut_windows(rows_ref, begin_ref, out_ref):
    def group(number, carry):
        here = pl.ds(pl.multiple_of(number * 16, 16), 16)
        begin = begin_ref[here, :]
        block = lax.shift_right_logical(begin, 7)
        rest = begin & 127
        lane = iota((16, 128), 1)
        values = []
        for source in range(PLANE):
            pair = rows_ref[source, here, :].astype(F32)
            values += [pair[:, :128], pair[:, 128:]]
        for bit, count in ((32, 64), (16, 48), (8, 40), (4, 36), (2, 34), (1, 33)):
            on = (block & bit) != 0
            values = [
                jnp.where(on, values[j + bit], values[j]) if j + bit < len(values) else values[j]
                for j in range(count)
            ]
        index = (lane + rest) & 127
        keep = lane + rest < 128
        moved = [jnp.take_along_axis(v, index, axis=1) for v in values]
        for j in range(32):
            piece = jnp.where(keep, moved[j], moved[j + 1]).astype(BF16)
            at = pl.ds(pl.multiple_of((j // 8) * 64 + number * 16, 16), 16)
            out_ref[at, (j % 8) * 128 : (j % 8) * 128 + 128] = piece
        return carry

    lax.fori_loop(0, 4, group, 0)


def coded(block):
    top = jnp.maximum(jnp.max(jnp.abs(block), axis=0, keepdims=True), 1e-30)
    return jnp.round(block * (TOP / top)).astype(I16), top * (1.0 / TOP)


def decoded(number_ref, scale_ref, index):
    return number_ref[index].astype(F32) * scale_ref[index]


def kernel(
    scale,
    head_ref, flow_ref, imp_ref, fric_ref, junc_ref, count_ref, kind_ref, up_ref, down_ref, open_ref, begin_ref,
    weights_ref,
    end_ref, grads_ref,
    head, flow, weights, prm, halo_out, halo_in, heads, flows, h1, q1, turned, head_end,
    start_rows, end_rows, begin, a0, a1, z_val, out_val, targets, at_own, at_in, g_own, g_in,
    d_sum, sa, sas, ra, ras, sb, sbs, rb, rbs, a_sum, b_sum, sa2, sa2s, ra2, ra2s, sb2, sb2s, rb2, rb2s,
    z_sum, sz, szs, rz, rzs,
    lsem, hsend, hrecv, send1, recv1, send2, recv2, csend, crecv, rsend, rrecv,
):
    seg, samp, zpos = lax.axis_index("seg"), lax.axis_index("samp"), lax.axis_index("dp")
    y, xlo, core = seg // 4, (seg // 2) % 2, seg % 2
    x = samp * 2 + xlo
    position = seg * 2 + samp

    def at_plane(t):
        return {"seg": t // 2, "samp": t % 2}

    def at_x(t):
        return {"seg": y * 4 + (t % 2) * 2 + core, "samp": t // 2}

    def at_y(t):
        return {"seg": t * 4 + xlo * 2 + core}

    def at_z(t):
        return {"dp": t}

    at_core = {"seg": y * 4 + xlo * 2 + 1 - core}

    def remote(src, dst, send, recv, device):
        return pltpu.make_async_remote_copy(
            src_ref=src, dst_ref=dst, send_sem=send, recv_sem=recv, device_id=device, device_id_type=MESH
        )

    load_head = pltpu.make_async_copy(head_ref, head, lsem.at[0])
    load_flow = pltpu.make_async_copy(flow_ref, flow, lsem.at[1])
    load_weights = pltpu.make_async_copy(weights_ref, weights, lsem.at[2])
    load_head.start()
    load_flow.start()
    load_weights.start()

    barrier = pltpu.get_barrier_semaphore()

    def greet(p, c):
        pl.semaphore_signal(barrier, inc=1, device_id=at_plane((position + p) % PLANE), device_id_type=MESH)
        return c

    lax.fori_loop(1, PLANE, greet, 0)

    def greet_z(p, c):
        pl.semaphore_signal(barrier, inc=1, device_id=at_z((zpos + p) % 8), device_id_type=MESH)
        return c

    lax.fori_loop(1, 8, greet_z, 0)

    prepare_params(position, imp_ref, fric_ref, junc_ref, count_ref, kind_ref, up_ref, down_ref, open_ref, prm)
    lanes = pl.ds(pl.multiple_of((position // 2) * 128, 128), 128)
    own_begin = jnp.broadcast_to(begin_ref[:, lanes].astype(F32), (64, 128))
    chosen = iota((64, 128), 1) == iota((64, 128), 0) + (position % 2) * 64
    own_begin = jnp.sum(jnp.where(chosen, own_begin, 0.0), axis=1, keepdims=True)
    begin[...] = jnp.broadcast_to(own_begin, (64, 128)).astype(jnp.int32)

    halo_out[...] = jnp.zeros_like(halo_out)
    load_head.wait()
    load_flow.wait()
    unit = eye(256)

    def turn(t, c):
        rows = pl.ds(pl.multiple_of(t * 128, 128), 128)
        heads[t, 8:264, :] = dot(unit, head[rows, :], 1, 1)
        flows[t, 8:264, :] = dot(unit, flow[rows, :], 1, 1)
        lanes = pl.ds(pl.multiple_of(t * 128, 128), 128)
        halo_out[0, 0:2, lanes] = heads[t, 8:10, :]
        halo_out[0, 2:4, lanes] = flows[t, 8:10, :]
        halo_out[1, 0:2, lanes] = heads[t, 262:264, :]
        halo_out[1, 2:4, lanes] = flows[t, 262:264, :]
        return c

    lax.fori_loop(0, 16, turn, 0)

    pl.semaphore_wait(barrier, 38)

    below, above = (position + PLANE - 1) % PLANE, (position + 1) % PLANE
    halos = [
        remote(halo_out.at[0], halo_in.at[0], hsend.at[0], hrecv.at[0], at_plane(below)),
        remote(halo_out.at[1], halo_in.at[1], hsend.at[1], hrecv.at[1], at_plane(above)),
    ]
    for c in halos:
        c.start()

    def block(t):
        return pl.ds(pl.multiple_of(t * 64, 64), 64)

    def spread(source, target, send, recv, p):
        t = (position + p) % PLANE
        return remote(source.at[block(t)], target.at[position], send.at[p], recv.at[p], at_plane(t))

    def send_old(p, c):
        spread(head, start_rows, send1, recv1, p).start()
        return c

    lax.fori_loop(1, PLANE, send_old, 0)
    keep_old = pltpu.make_async_copy(head.at[block(position)], start_rows.at[position], lsem.at[3])
    keep_old.start()

    for c in halos:
        c.wait()

    small = eye(128)

    def one_tile(i, c):
        tile = (position // 2 + i) % 16
        lanes = pl.ds(pl.multiple_of(tile * 128, 128), 128)
        heads[tile, 264:266, :] = halo_in[0, 0:2, lanes]
        flows[tile, 264:266, :] = halo_in[0, 2:4, lanes]
        heads[tile, 6:8, :] = halo_in[1, 0:2, lanes]
        flows[tile, 6:8, :] = halo_in[1, 2:4, lanes]
        stencil_tile(position, tile, prm, heads, flows, h1, q1, turned)
        head_end[pl.ds(pl.multiple_of(tile * 128, 128), 128), :] = dot(small, turned[...], 1, 1).astype(BF16)
        for k in range(2):
            t = 2 * tile + k
            p = (t - position + PLANE) % PLANE

            @pl.when(p > 0)
            def _():
                spread(head_end, end_rows, send2, recv2, p).start()

        return c

    lax.fori_loop(0, 16, one_tile, 0)
    keep_new = pltpu.make_async_copy(head_end.at[block(position)], end_rows.at[position], lsem.at[4])
    keep_new.start()
    store_end = pltpu.make_async_copy(head_end, end_ref, lsem.at[5])
    store_end.start()

    load_weights.wait()
    keep_old.wait()

    def wait_old(p, c):
        spread(head, start_rows, send1, recv1, p).wait()
        return c

    lax.fori_loop(1, PLANE, wait_old, 0)
    cut_windows(start_rows, begin, a0)
    for c in range(4):
        cols = slice(c * 256, c * 256 + 256)
        z = dot(a0[...], weights[0, :, cols], 1, 0)
        z_val[:, cols] = z
        a1[:, cols] = (z * jax.nn.sigmoid(z)).astype(BF16)
    for c in range(4):
        cols = slice(c * 256, c * 256 + 256)
        out_val[:, cols] = dot(a1[...], weights[1, :, cols], 1, 0)

    def turn_a(b, c):
        cols = pl.ds(pl.multiple_of(b * 128, 128), 128)
        for layer, source in ((0, a0), (1, a1)):
            both = source[:, cols].T
            at_own[layer, b, 0] = both[0:64]
            at_own[layer, b, 1] = both[64:128]
        return c

    lax.fori_loop(0, 8, turn_a, 0)
    core_a = remote(at_own.at[:, :, 1 - core], at_in, csend.at[0], crecv.at[0], at_core)
    core_a.start()

    keep_new.wait()

    def wait_new(p, c):
        spread(head_end, end_rows, send2, recv2, p).wait()
        return c

    lax.fori_loop(1, PLANE, wait_new, 0)
    cut_windows(end_rows, begin, targets)
    g_own[1] = ((out_val[...] - targets[...].astype(F32)) * scale).astype(BF16)
    core_g1 = remote(g_own.at[1], g_in.at[1], csend.at[1], crecv.at[1], at_core)
    core_g1.start()
    for c in range(4):
        cols = slice(c * 256, c * 256 + 256)
        back = dot(g_own[1], weights[1, cols, :], 1, 1)
        z = z_val[:, cols]
        sigma = jax.nn.sigmoid(z)
        g_own[0, :, cols] = (back * sigma * (1.0 + z * (1.0 - sigma))).astype(BF16)
    core_g0 = remote(g_own.at[0], g_in.at[0], csend.at[2], crecv.at[2], at_core)
    core_g0.start()
    core_a.wait()
    core_g1.wait()

    copies = []
    for layer in (1, 0):
        if layer == 0:
            core_g0.wait()

        def one_block(b, c, layer=layer):
            d = dot(at_own[layer, b, core], g_own[layer], 1, 0) + dot(at_in[layer, b], g_in[layer], 1, 0)
            d_sum[layer * 8 + b] = d
            yy, xx = b // 2, b % 2
            for hi in range(2):
                numbers, scales = coded(d[hi * 32 : hi * 32 + 32, 0:512])
                sa[hi * 2 + xx, layer * 4 + yy] = numbers
                sas[hi * 2 + xx, layer * 4 + yy] = scales
                numbers, scales = coded(d[hi * 32 : hi * 32 + 32, 512:1024])
                sb[yy, layer * 4 + hi * 2 + xx] = numbers
                sbs[yy, layer * 4 + hi * 2 + xx] = scales
            return c

        lax.fori_loop(0, 8, one_block, 0)
        part = pl.ds(layer * 4, 4)
        for p in range(1, 4):
            tx, ty = (x + p) % 4, (y + p) % 4
            k = (layer * 3 + p - 1) * 4
            copies += [
                remote(sa.at[tx, part], ra.at[p - 1, part], rsend.at[k], rrecv.at[k], at_x(tx)),
                remote(sas.at[tx, part], ras.at[p - 1, part], rsend.at[k + 1], rrecv.at[k + 1], at_x(tx)),
                remote(sb.at[ty, part], rb.at[p - 1, part], rsend.at[k + 2], rrecv.at[k + 2], at_y(ty)),
                remote(sbs.at[ty, part], rbs.at[p - 1, part], rsend.at[k + 3], rrecv.at[k + 3], at_y(ty)),
            ]
        for c in copies[-12:]:
            c.start()
    for c in copies:
        c.wait()

    own_rows = pl.ds(pl.multiple_of(samp * 32, 32), 32)

    def add_first(i, c):
        layer, rest = i // 4, i % 4
        left = d_sum[layer * 8 + rest * 2 + xlo, own_rows, 0:512]
        high = pl.ds(pl.multiple_of((rest // 2) * 32, 32), 32)
        right = d_sum[layer * 8 + y * 2 + rest % 2, high, 512:1024]
        for p in range(3):
            left = left + ra[p, i].astype(F32) * ras[p, i]
            right = right + rb[p, i].astype(F32) * rbs[p, i]
        a_sum[i] = left
        b_sum[i] = right
        sa2[rest, layer], sa2s[rest, layer] = coded(left)
        sb2[rest, layer], sb2s[rest, layer] = coded(right)
        return c

    lax.fori_loop(0, 8, add_first, 0)
    copies = []
    for p in range(1, 4):
        tx, ty = (x + p) % 4, (y + p) % 4
        k = 24 + (p - 1) * 4
        copies += [
            remote(sa2.at[ty], ra2.at[p - 1], rsend.at[k], rrecv.at[k], at_y(ty)),
            remote(sa2s.at[ty], ra2s.at[p - 1], rsend.at[k + 1], rrecv.at[k + 1], at_y(ty)),
            remote(sb2.at[tx], rb2.at[p - 1], rsend.at[k + 2], rrecv.at[k + 2], at_x(tx)),
            remote(sb2s.at[tx], rb2s.at[p - 1], rsend.at[k + 3], rrecv.at[k + 3], at_x(tx)),
        ]
    for c in copies:
        c.start()
    for c in copies:
        c.wait()

    for layer in range(2):
        left = a_sum[layer * 4 + y]
        right = b_sum[layer * 4 + x]
        for p in range(3):
            left = left + ra2[p, layer].astype(F32) * ra2s[p, layer]
            right = right + rb2[p, layer].astype(F32) * rb2s[p, layer]
        for t in range(8):
            z_sum[t, 4 * layer : 4 * layer + 4] = left[4 * t : 4 * t + 4]
            z_sum[t, 8 + 4 * layer : 12 + 4 * layer] = right[4 * t : 4 * t + 4]
    for t in range(8):
        sz[t], szs[t] = coded(z_sum[t])
    copies = []
    for p in range(1, 8):
        t = (zpos + p) % 8
        k = 36 + (p - 1) * 2
        copies += [
            remote(sz.at[t], rz.at[p - 1], rsend.at[k], rrecv.at[k], at_z(t)),
            remote(szs.at[t], rzs.at[p - 1], rsend.at[k + 1], rrecv.at[k + 1], at_z(t)),
        ]
    for c in copies:
        c.start()
    for c in copies:
        c.wait()
    total = z_sum[zpos]
    for p in range(7):
        total = total + rz[p].astype(F32) * rzs[p]
    for layer in range(2):
        grads_ref[layer, :, 0:512] = total[4 * layer : 4 * layer + 4]
        grads_ref[layer, :, 512:1024] = total[8 + 4 * layer : 12 + 4 * layer]
    store_end.wait()


def whole(scale, *operands):
    hbm = pl.BlockSpec(memory_space=pl.ANY)
    vmem = pl.BlockSpec(memory_space=pltpu.VMEM)
    dma = pltpu.SemaphoreType.DMA
    return pl.pallas_call(
        functools.partial(kernel, scale),
        out_shape=[
            jax.ShapeDtypeStruct((2048, 256), BF16),
            jax.ShapeDtypeStruct((2, 4, 1024), F32),
        ],
        in_specs=[hbm, hbm] + [vmem] * 9 + [hbm],
        out_specs=[hbm, vmem],
        scratch_shapes=[
            pltpu.VMEM((2048, 256), BF16),
            pltpu.VMEM((2048, 256), BF16),
            pltpu.VMEM((2, 1024, 1024), BF16),
            pltpu.VMEM((16, 2048), F32),
            pltpu.VMEM((2, 8, 2048), F32),
            pltpu.VMEM((2, 8, 2048), F32),
            pltpu.VMEM((16, 272, 128), F32),
            pltpu.VMEM((16, 272, 128), F32),
            pltpu.VMEM((264, 128), F32),
            pltpu.VMEM((264, 128), F32),
            pltpu.VMEM((256, 128), BF16),
            pltpu.VMEM((2048, 256), BF16),
            pltpu.VMEM((32, 64, 256), BF16),
            pltpu.VMEM((32, 64, 256), BF16),
            pltpu.VMEM((64, 128), jnp.int32),
            pltpu.VMEM((256, 1024), BF16),
            pltpu.VMEM((256, 1024), BF16),
            pltpu.VMEM((256, 1024), F32),
            pltpu.VMEM((256, 1024), F32),
            pltpu.VMEM((256, 1024), BF16),
            pltpu.VMEM((2, 8, 2, 64, 256), BF16),
            pltpu.VMEM((2, 8, 64, 256), BF16),
            pltpu.VMEM((2, 256, 1024), BF16),
            pltpu.VMEM((2, 256, 1024), BF16),
            pltpu.VMEM((16, 64, 1024), F32),
            pltpu.VMEM((4, 8, 32, 512), I16),
            pltpu.VMEM((4, 8, 1, 512), F32),
            pltpu.VMEM((3, 8, 32, 512), I16),
            pltpu.VMEM((3, 8, 1, 512), F32),
            pltpu.VMEM((4, 8, 32, 512), I16),
            pltpu.VMEM((4, 8, 1, 512), F32),
            pltpu.VMEM((3, 8, 32, 512), I16),
            pltpu.VMEM((3, 8, 1, 512), F32),
            pltpu.VMEM((8, 32, 512), F32),
            pltpu.VMEM((8, 32, 512), F32),
            pltpu.VMEM((4, 2, 32, 512), I16),
            pltpu.VMEM((4, 2, 1, 512), F32),
            pltpu.VMEM((3, 2, 32, 512), I16),
            pltpu.VMEM((3, 2, 1, 512), F32),
            pltpu.VMEM((4, 2, 32, 512), I16),
            pltpu.VMEM((4, 2, 1, 512), F32),
            pltpu.VMEM((3, 2, 32, 512), I16),
            pltpu.VMEM((3, 2, 1, 512), F32),
            pltpu.VMEM((8, 16, 512), F32),
            pltpu.VMEM((8, 16, 512), I16),
            pltpu.VMEM((8, 1, 512), F32),
            pltpu.VMEM((7, 16, 512), I16),
            pltpu.VMEM((7, 1, 512), F32),
            dma((8,)),
            dma((2,)),
            dma((2,)),
            dma((PLANE,)),
            dma((PLANE,)),
            dma((PLANE,)),
            dma((PLANE,)),
            dma((3,)),
            dma((3,)),
            dma((50,)),
            dma((50,)),
        ],
        compiler_params=pltpu.CompilerParams(
            collective_id=1, has_side_effects=True, vmem_limit_bytes=58 << 20
        ),
    )(*operands)


def body(
    head_start,
    flow_start,
    impedance,
    friction,
    seg_count,
    junction_code,
    boundary_code,
    head_up,
    head_down,
    opening,
    window_start,
    layer_weights,
):
    row_total = window_start.shape[0] * lax.axis_size("dp") * 4
    return tuple(
        whole(
            8.0 / row_total,
            head_start,
            flow_start,
            impedance.T,
            friction.T,
            junction_code.T,
            seg_count[None, :],
            boundary_code[None, :],
            head_up[None, :],
            head_down[None, :],
            opening[None, :],
            window_start[None, :],
            layer_weights,
        )
    )


def solution(mesh):
    placed = (
        P("dp", ("seg", "samp")),
        P("dp", ("seg", "samp")),
        P("dp", None),
        P("dp", None),
        P("dp"),
        P("dp", None),
        P("dp"),
        P("dp"),
        P("dp"),
        P("dp"),
        P("dp"),
        P(),
    )
    return jax.shard_map(
        body,
        mesh=mesh,
        in_specs=placed,
        out_specs=(P("dp", ("seg", "samp")), P(None, ("seg", "samp", "dp"), None)),
        check_vma=False,
    )
```

```python
import functools
import jax
import jax.numpy as jnp
from jax import lax
from jax.experimental import pallas as pl
from jax.experimental.pallas import tpu as pltpu
from jax.sharding import PartitionSpec as P

MESH = pl.DeviceIdType.MESH
PLANE = 32
CELLS = 8192
BF16 = jnp.bfloat16
F32 = jnp.float32
I16 = jnp.int16
TOP = 32767.0


def dot(lhs, rhs, lhs_dim, rhs_dim):
    return lax.dot_general(
        lhs, rhs, (((lhs_dim,), (rhs_dim,)), ((), ())), preferred_element_type=F32
    )


def iota(shape, dim):
    return lax.broadcasted_iota(jnp.int32, shape, dim)


def far_first():
    offsets = [(dy, dx, dc) for dy in range(4) for dx in range(4) for dc in range(2)][1:]

    def key(offset):
        dy, dx, dc = offset
        return (min(dy, 4 - dy) + min(dx, 4 - dx), dc, (dx * 7 + dy * 3) % 5)

    return sorted(offsets, key=key, reverse=True)


def eye(size):
    return jnp.where(iota((size, size), 0) == iota((size, size), 1), 1.0, 0.0).astype(BF16)


W_LO, W_HI, L_LO, L_HI, H_LO, H_HI, FIRST, COUNT, END_A, END_L, END_Q, UPPER = range(12)


def prepare_params(position, imp_ref, fric_ref, junc_ref, count_ref, kind_ref, up_ref, down_ref, open_ref, prm):
    wide = imp_ref.shape
    imp = imp_ref[...]
    loss = fric_ref[...] * (1.0 + junc_ref[...].astype(F32))
    count = count_ref[...]
    before = position * 256 - 1
    section = lax.shift_right_logical(jnp.maximum(before, 0) * count, 13)
    row = iota(wide, 0)

    def pick(values, number):
        return jnp.sum(jnp.where(row == number, values, 0.0), axis=0, keepdims=True)

    w_lo, w_hi = pick(imp, section), pick(imp, section + 1)
    w_end = pick(imp, count - 1)
    prm[W_LO : W_LO + 1] = w_lo
    prm[W_HI : W_HI + 1] = w_hi
    prm[L_LO : L_LO + 1] = pick(loss, section)
    prm[L_HI : L_HI + 1] = pick(loss, section + 1)
    prm[H_LO : H_LO + 1] = 0.5 / w_lo
    prm[H_HI : H_HI + 1] = 0.5 / jnp.where(w_hi == 0.0, 1.0, w_hi)
    prm[FIRST : FIRST + 1] = (before * count - (section + 1) * CELLS).astype(F32)
    prm[COUNT : COUNT + 1] = count.astype(F32)
    kind, valve = kind_ref[...], open_ref[...]
    factor = 1.0 / (1.0 + w_end * valve)
    prm[END_A : END_A + 1] = jnp.where(kind == 0, 0.0, jnp.where(kind == 1, 1.0, factor))
    prm[END_L : END_L + 1] = jnp.where(kind == 0, down_ref[...], 0.0)
    prm[END_Q : END_Q + 1] = jnp.where(kind == 0, 1.0 / w_end, jnp.where(kind == 1, 0.0, valve * factor))
    prm[UPPER : UPPER + 1] = up_ref[...]


def stencil_tile(position, tile, prm, heads, flows, h1, q1, turned):
    lanes = pl.ds(pl.multiple_of(tile * 128, 128), 128)

    def param(number, rows=8):
        return jnp.broadcast_to(prm[number : number + 1, lanes], (rows, 128))

    count = param(COUNT)
    start = param(FIRST) + iota((8, 128), 0).astype(F32) * count
    lows = [param(W_LO), param(L_LO), param(H_LO)]
    highs = [param(W_HI), param(L_HI), param(H_HI)]

    def fields(value, number):
        high = value >= 0.0
        return [jnp.where(high, highs[k], lows[k]) for k in range(number)]

    def ends(lh, lq, rh, rq, wave, loss):
        forward = lh + lq * (wave - loss * jnp.abs(lq))
        backward = rh - rq * (wave - loss * jnp.abs(rq))
        return forward, backward

    def first(g, value):
        wave, loss, half = fields(value, 3)
        left, right = pl.ds(8 * g + 6, 8), pl.ds(8 * g + 8, 8)
        forward, backward = ends(
            heads[tile, left, :], flows[tile, left, :], heads[tile, right, :], flows[tile, right, :], wave, loss
        )
        return forward, backward, half

    value = start
    for g in range(33):
        forward, backward, half = first(g, value)
        h1[8 * g : 8 * g + 8] = 0.5 * (forward + backward)
        q1[8 * g : 8 * g + 8] = (forward - backward) * half
        value = value + 8.0 * count

    @pl.when(position == 0)
    def _():
        _, backward, half = first(0, start)
        upper = param(UPPER)
        at = iota((8, 128), 0) == 1
        h1[0:8] = jnp.where(at, upper, h1[0:8])
        q1[0:8] = jnp.where(at, (upper - backward) * (2.0 * half), q1[0:8])

    @pl.when(position == PLANE - 1)
    def _():
        forward, _, _ = first(32, start + 256.0 * count)
        at = iota((8, 128), 0) == 0
        h1[256:264] = jnp.where(at, param(END_A) * forward + param(END_L), h1[256:264])
        q1[256:264] = jnp.where(at, (forward - param(END_L)) * param(END_Q), q1[256:264])

    def second(g, value):
        wave, loss = fields(value, 2)
        left, right = pl.ds(8 * g, 8), pl.ds(8 * g + 2, 8)
        return ends(h1[left, :], q1[left, :], h1[right, :], q1[right, :], wave, loss)

    value = start + count
    for g in range(16):
        pieces = []
        for _ in range(2):
            forward, backward = second(2 * g + len(pieces), value)
            pieces.append(0.5 * (forward + backward))
            value = value + 8.0 * count
        turned[16 * g : 16 * g + 16] = jnp.concatenate(pieces, axis=0).astype(BF16)

    @pl.when(position == 0)
    def _():
        at = iota((16, 128), 0) == 0
        turned[0:16] = jnp.where(at, param(UPPER, 16), turned[0:16].astype(F32)).astype(BF16)

    @pl.when(position == PLANE - 1)
    def _():
        forward, _ = second(31, start + 249.0 * count)
        last = param(END_A) * forward + param(END_L)
        last = jnp.concatenate([last, last], axis=0)
        at = iota((16, 128), 0) == 15
        turned[240:256] = jnp.where(at, last, turned[240:256].astype(F32)).astype(BF16)


def cut_windows(rows_ref, begin_ref, out_ref):
    def group(number, carry):
        here = pl.ds(pl.multiple_of(number * 16, 16), 16)
        begin = begin_ref[here, :]
        block = lax.shift_right_logical(begin, 7)
        rest = begin & 127
        lane = iota((16, 128), 1)
        values = []
        for source in range(PLANE):
            pair = rows_ref[source, here, :].astype(F32)
            values += [pair[:, :128], pair[:, 128:]]
        for bit, count in ((32, 64), (16, 48), (8, 40), (4, 36), (2, 34), (1, 33)):
            on = (block & bit) != 0
            values = [
                jnp.where(on, values[j + bit], values[j]) if j + bit < len(values) else values[j]
                for j in range(count)
            ]
        index = (lane + rest) & 127
        keep = lane + rest < 128
        moved = [jnp.take_along_axis(v, index, axis=1) for v in values]
        for j in range(32):
            piece = jnp.where(keep, moved[j], moved[j + 1]).astype(BF16)
            at = pl.ds(pl.multiple_of((j // 8) * 64 + number * 16, 16), 16)
            out_ref[at, (j % 8) * 128 : (j % 8) * 128 + 128] = piece
        return carry

    lax.fori_loop(0, 4, group, 0)


def coded(block):
    top = jnp.maximum(jnp.max(jnp.abs(block), axis=0, keepdims=True), 1e-30)
    return jnp.round(block * (TOP / top)).astype(I16), top * (1.0 / TOP)


def decoded(number_ref, scale_ref, index):
    return number_ref[index].astype(F32) * scale_ref[index]


def kernel(
    scale,
    head_ref, flow_ref, imp_ref, fric_ref, junc_ref, count_ref, kind_ref, up_ref, down_ref, open_ref, begin_ref,
    weights_ref,
    end_ref, grads_ref,
    head, flow, weights, prm, halo_out, halo_in, heads, flows, h1, q1, turned, head_end,
    start_rows, end_rows, begin, a0, a1, z_val, out_val, targets, at_own, at_in, g_own, g_in,
    d_sum, sa, sas, ra, ras, sb, sbs, rb, rbs, a_sum, b_sum, sa2, sa2s, ra2, ra2s, sb2, sb2s, rb2, rb2s,
    z_sum, sz, szs, rz, rzs,
    lsem, hsend, hrecv, send1, recv1, send2, recv2, csend, crecv, rsend, rrecv,
):
    seg, samp, zpos = lax.axis_index("seg"), lax.axis_index("samp"), lax.axis_index("dp")
    y, xlo, core = seg // 4, (seg // 2) % 2, seg % 2
    x = samp * 2 + xlo
    position = seg * 2 + samp

    def at_plane(t):
        return {"seg": t // 2, "samp": t % 2}

    def at_x(t):
        return {"seg": y * 4 + (t % 2) * 2 + core, "samp": t // 2}

    def at_y(t):
        return {"seg": t * 4 + xlo * 2 + core}

    def at_z(t):
        return {"dp": t}

    at_core = {"seg": y * 4 + xlo * 2 + 1 - core}

    def remote(src, dst, send, recv, device):
        return pltpu.make_async_remote_copy(
            src_ref=src, dst_ref=dst, send_sem=send, recv_sem=recv, device_id=device, device_id_type=MESH
        )

    load_head = pltpu.make_async_copy(head_ref, head, lsem.at[0])
    load_flow = pltpu.make_async_copy(flow_ref, flow, lsem.at[1])
    load_weights = pltpu.make_async_copy(weights_ref, weights, lsem.at[2])
    load_head.start()
    load_flow.start()
    load_weights.start()

    barrier = pltpu.get_barrier_semaphore()

    def greet(p, c):
        pl.semaphore_signal(barrier, inc=1, device_id=at_plane((position + p) % PLANE), device_id_type=MESH)
        return c

    lax.fori_loop(1, PLANE, greet, 0)

    def greet_z(p, c):
        pl.semaphore_signal(barrier, inc=1, device_id=at_z((zpos + p) % 8), device_id_type=MESH)
        return c

    lax.fori_loop(1, 8, greet_z, 0)

    row, lane = iota((16, 256), 0), iota((16, 256), 1)
    pick = jnp.where((row < 4) & (lane == jnp.where(row < 2, row, row + 252)), 1.0, 0.0).astype(BF16)
    halo_out[...] = jnp.zeros_like(halo_out)
    load_head.wait()
    edge = dot(pick, head[...], 1, 1)
    halo_out[0, 0:2] = edge[0:2]
    halo_out[1, 0:2] = edge[2:4]
    load_flow.wait()
    edge = dot(pick, flow[...], 1, 1)
    halo_out[0, 2:4] = edge[0:2]
    halo_out[1, 2:4] = edge[2:4]

    pl.semaphore_wait(barrier, 38)

    below, above = (position + PLANE - 1) % PLANE, (position + 1) % PLANE
    halos = [
        remote(halo_out.at[0], halo_in.at[0], hsend.at[0], hrecv.at[0], at_plane(below)),
        remote(halo_out.at[1], halo_in.at[1], hsend.at[1], hrecv.at[1], at_plane(above)),
    ]
    for c in halos:
        c.start()

    def block(t):
        return pl.ds(pl.multiple_of(t * 64, 64), 64)

    def spread(source, target, send, recv, p):
        t = (position + p) % PLANE
        return remote(source.at[block(t)], target.at[position], send.at[p], recv.at[p], at_plane(t))

    for dy, dx, dc in far_first():
        tx = (x + dx) % 4
        t = ((y + dy) % 4) * 8 + (tx % 2) * 4 + ((core + dc) % 2) * 2 + tx // 2
        spread(head, start_rows, send1, recv1, (t - position + PLANE) % PLANE).start()
    keep_old = pltpu.make_async_copy(head.at[block(position)], start_rows.at[position], lsem.at[3])
    keep_old.start()

    prepare_params(position, imp_ref, fric_ref, junc_ref, count_ref, kind_ref, up_ref, down_ref, open_ref, prm)
    lanes = pl.ds(pl.multiple_of((position // 2) * 128, 128), 128)
    own_begin = jnp.broadcast_to(begin_ref[:, lanes].astype(F32), (64, 128))
    chosen = iota((64, 128), 1) == iota((64, 128), 0) + (position % 2) * 64
    own_begin = jnp.sum(jnp.where(chosen, own_begin, 0.0), axis=1, keepdims=True)
    begin[...] = jnp.broadcast_to(own_begin, (64, 128)).astype(jnp.int32)
    unit = eye(256)

    def turn(t, c):
        rows = pl.ds(pl.multiple_of(t * 128, 128), 128)
        heads[t, 8:264, :] = dot(unit, head[rows, :], 1, 1)
        flows[t, 8:264, :] = dot(unit, flow[rows, :], 1, 1)
        return c

    lax.fori_loop(0, 16, turn, 0)
    for c in halos:
        c.wait()

    small = eye(128)

    def one_tile(i, c):
        turn_y = i // 4
        turn_y = jnp.where(turn_y < 2, 2 - turn_y, 6 - turn_y)
        turn_y = jnp.where(i >= 12, 0, jnp.where(i >= 8, 3, turn_y))
        tile = ((y + turn_y) % 4) * 4 + (xlo * 2 + core + i) % 4
        lanes = pl.ds(pl.multiple_of(tile * 128, 128), 128)
        heads[tile, 264:266, :] = halo_in[0, 0:2, lanes]
        flows[tile, 264:266, :] = halo_in[0, 2:4, lanes]
        heads[tile, 6:8, :] = halo_in[1, 0:2, lanes]
        flows[tile, 6:8, :] = halo_in[1, 2:4, lanes]
        stencil_tile(position, tile, prm, heads, flows, h1, q1, turned)
        head_end[pl.ds(pl.multiple_of(tile * 128, 128), 128), :] = dot(small, turned[...], 1, 1).astype(BF16)
        for k in range(2):
            t = 2 * tile + k
            p = (t - position + PLANE) % PLANE

            @pl.when(p > 0)
            def _():
                spread(head_end, end_rows, send2, recv2, p).start()

        return c

    lax.fori_loop(0, 16, one_tile, 0)
    keep_new = pltpu.make_async_copy(head_end.at[block(position)], end_rows.at[position], lsem.at[4])
    keep_new.start()
    store_end = pltpu.make_async_copy(head_end, end_ref, lsem.at[5])
    store_end.start()

    load_weights.wait()
    keep_old.wait()

    def wait_old(p, c):
        spread(head, start_rows, send1, recv1, p).wait()
        return c

    lax.fori_loop(1, PLANE, wait_old, 0)
    cut_windows(start_rows, begin, a0)
    for c in range(4):
        cols = slice(c * 256, c * 256 + 256)
        z = dot(a0[...], weights[0, :, cols], 1, 0)
        z_val[:, cols] = z
        a1[:, cols] = (z * jax.nn.sigmoid(z)).astype(BF16)
    for c in range(4):
        cols = slice(c * 256, c * 256 + 256)
        out_val[:, cols] = dot(a1[...], weights[1, :, cols], 1, 0)

    def turn_a(b, c):
        cols = pl.ds(pl.multiple_of(b * 128, 128), 128)
        for layer, source in ((0, a0), (1, a1)):
            both = source[:, cols].T
            at_own[layer, 0, b] = both[0:64]
            at_own[layer, 1, b] = both[64:128]
        return c

    lax.fori_loop(0, 8, turn_a, 0)
    core_a = remote(at_own.at[:, 1 - core], at_in, csend.at[0], crecv.at[0], at_core)
    core_a.start()

    keep_new.wait()

    def wait_new(p, c):
        spread(head_end, end_rows, send2, recv2, p).wait()
        return c

    lax.fori_loop(1, PLANE, wait_new, 0)
    cut_windows(end_rows, begin, targets)
    g_own[1] = ((out_val[...] - targets[...].astype(F32)) * scale).astype(BF16)
    core_g1 = remote(g_own.at[1], g_in.at[1], csend.at[1], crecv.at[1], at_core)
    core_g1.start()
    for c in range(4):
        cols = slice(c * 256, c * 256 + 256)
        back = dot(g_own[1], weights[1, cols, :], 1, 1)
        z = z_val[:, cols]
        sigma = jax.nn.sigmoid(z)
        g_own[0, :, cols] = (back * sigma * (1.0 + z * (1.0 - sigma))).astype(BF16)
    core_g0 = remote(g_own.at[0], g_in.at[0], csend.at[2], crecv.at[2], at_core)
    core_g0.start()
    core_a.wait()
    core_g1.wait()

    firsts = {}
    for layer in (1, 0):
        if layer == 0:
            core_g0.wait()
        part = pl.ds(layer * 4, 4)
        blocks = pl.ds(layer * 8, 8)
        for side in range(2):
            for c in (2 * side, 2 * side + 1):
                cols = slice(c * 256, c * 256 + 256)
                d = dot(at_own[layer, core].reshape(512, 256), g_own[layer, :, cols], 1, 0)
                d = d + dot(at_in[layer].reshape(512, 256), g_in[layer, :, cols], 1, 0)
                d_sum[blocks, :, cols] = d.reshape(8, 64, 256)

            def code_left(b, c, layer=layer):
                yy, xx = b // 2, b % 2
                for hi in range(2):
                    numbers, scales = coded(d_sum[layer * 8 + b, hi * 32 : hi * 32 + 32, 0:512])
                    sa[hi * 2 + xx, layer * 4 + yy] = numbers
                    sas[hi * 2 + xx, layer * 4 + yy] = scales
                return c

            def code_right(b, c, layer=layer):
                yy, xx = b // 2, b % 2
                for hi in range(2):
                    numbers, scales = coded(d_sum[layer * 8 + b, hi * 32 : hi * 32 + 32, 512:1024])
                    sb[yy, layer * 4 + hi * 2 + xx] = numbers
                    sbs[yy, layer * 4 + hi * 2 + xx] = scales
                return c

            lax.fori_loop(0, 8, code_right if side else code_left, 0)
            copies = []
            for p in (2, 1, 3):
                tx, ty = (x + p) % 4, (y + p) % 4
                k = ((layer * 2 + side) * 3 + p - 1) * 2
                if side == 0:
                    copies += [
                        remote(sa.at[tx, part], ra.at[p - 1, part], rsend.at[k], rrecv.at[k], at_x(tx)),
                        remote(sas.at[tx, part], ras.at[p - 1, part], rsend.at[k + 1], rrecv.at[k + 1], at_x(tx)),
                    ]
                else:
                    copies += [
                        remote(sb.at[ty, part], rb.at[p - 1, part], rsend.at[k], rrecv.at[k], at_y(ty)),
                        remote(sbs.at[ty, part], rbs.at[p - 1, part], rsend.at[k + 1], rrecv.at[k + 1], at_y(ty)),
                    ]
            for c in copies:
                c.start()
            firsts[layer, side] = copies

    own_rows = pl.ds(pl.multiple_of(samp * 32, 32), 32)
    seconds = []
    for layer in (1, 0):
        for side in range(2):
            for c in firsts[layer, side]:
                c.wait()

            def add_left(rest, c, layer=layer):
                i = layer * 4 + rest
                left = d_sum[layer * 8 + rest * 2 + xlo, own_rows, 0:512]
                for p in range(3):
                    left = left + ra[p, i].astype(F32) * ras[p, i]
                a_sum[i] = left
                sa2[rest, layer], sa2s[rest, layer] = coded(left)
                return c

            def add_right(rest, c, layer=layer):
                i = layer * 4 + rest
                high = pl.ds(pl.multiple_of((rest // 2) * 32, 32), 32)
                right = d_sum[layer * 8 + y * 2 + rest % 2, high, 512:1024]
                for p in range(3):
                    right = right + rb[p, i].astype(F32) * rbs[p, i]
                b_sum[i] = right
                sb2[rest, layer], sb2s[rest, layer] = coded(right)
                return c

            lax.fori_loop(0, 4, add_right if side else add_left, 0)
            copies = []
            for p in (2, 1, 3):
                tx, ty = (x + p) % 4, (y + p) % 4
                k = 24 + ((layer * 2 + side) * 3 + p - 1) * 2
                if side == 0:
                    copies += [
                        remote(sa2.at[ty, layer], ra2.at[p - 1, layer], rsend.at[k], rrecv.at[k], at_y(ty)),
                        remote(sa2s.at[ty, layer], ra2s.at[p - 1, layer], rsend.at[k + 1], rrecv.at[k + 1], at_y(ty)),
                    ]
                else:
                    copies += [
                        remote(sb2.at[tx, layer], rb2.at[p - 1, layer], rsend.at[k], rrecv.at[k], at_x(tx)),
                        remote(sb2s.at[tx, layer], rb2s.at[p - 1, layer], rsend.at[k + 1], rrecv.at[k + 1], at_x(tx)),
                    ]
            for c in copies:
                c.start()
            seconds += copies
    for c in seconds:
        c.wait()

    for layer in range(2):
        left = a_sum[layer * 4 + y]
        right = b_sum[layer * 4 + x]
        for p in range(3):
            left = left + ra2[p, layer].astype(F32) * ra2s[p, layer]
            right = right + rb2[p, layer].astype(F32) * rb2s[p, layer]
        for t in range(8):
            z_sum[t, 4 * layer : 4 * layer + 4] = left[4 * t : 4 * t + 4]
            z_sum[t, 8 + 4 * layer : 12 + 4 * layer] = right[4 * t : 4 * t + 4]
    for t in range(8):
        sz[t], szs[t] = coded(z_sum[t])
    copies = []
    for p in (4, 3, 5, 2, 6, 1, 7):
        t = (zpos + p) % 8
        k = 48 + (p - 1) * 2
        copies += [
            remote(sz.at[t], rz.at[p - 1], rsend.at[k], rrecv.at[k], at_z(t)),
            remote(szs.at[t], rzs.at[p - 1], rsend.at[k + 1], rrecv.at[k + 1], at_z(t)),
        ]
    for c in copies:
        c.start()
    for c in copies:
        c.wait()
    total = z_sum[zpos]
    for p in range(7):
        total = total + rz[p].astype(F32) * rzs[p]
    for layer in range(2):
        grads_ref[layer, :, 0:512] = total[4 * layer : 4 * layer + 4]
        grads_ref[layer, :, 512:1024] = total[8 + 4 * layer : 12 + 4 * layer]
    store_end.wait()


def whole(scale, *operands):
    hbm = pl.BlockSpec(memory_space=pl.ANY)
    vmem = pl.BlockSpec(memory_space=pltpu.VMEM)
    dma = pltpu.SemaphoreType.DMA
    return pl.pallas_call(
        functools.partial(kernel, scale),
        out_shape=[
            jax.ShapeDtypeStruct((2048, 256), BF16),
            jax.ShapeDtypeStruct((2, 4, 1024), F32),
        ],
        in_specs=[hbm, hbm] + [vmem] * 9 + [hbm],
        out_specs=[hbm, vmem],
        scratch_shapes=[
            pltpu.VMEM((2048, 256), BF16),
            pltpu.VMEM((2048, 256), BF16),
            pltpu.VMEM((2, 1024, 1024), BF16),
            pltpu.VMEM((16, 2048), F32),
            pltpu.VMEM((2, 8, 2048), F32),
            pltpu.VMEM((2, 8, 2048), F32),
            pltpu.VMEM((16, 272, 128), F32),
            pltpu.VMEM((16, 272, 128), F32),
            pltpu.VMEM((264, 128), F32),
            pltpu.VMEM((264, 128), F32),
            pltpu.VMEM((256, 128), BF16),
            pltpu.VMEM((2048, 256), BF16),
            pltpu.VMEM((32, 64, 256), BF16),
            pltpu.VMEM((32, 64, 256), BF16),
            pltpu.VMEM((64, 128), jnp.int32),
            pltpu.VMEM((256, 1024), BF16),
            pltpu.VMEM((256, 1024), BF16),
            pltpu.VMEM((256, 1024), F32),
            pltpu.VMEM((256, 1024), F32),
            pltpu.VMEM((256, 1024), BF16),
            pltpu.VMEM((2, 2, 8, 64, 256), BF16),
            pltpu.VMEM((2, 8, 64, 256), BF16),
            pltpu.VMEM((2, 256, 1024), BF16),
            pltpu.VMEM((2, 256, 1024), BF16),
            pltpu.VMEM((16, 64, 1024), F32),
            pltpu.VMEM((4, 8, 32, 512), I16),
            pltpu.VMEM((4, 8, 1, 512), F32),
            pltpu.VMEM((3, 8, 32, 512), I16),
            pltpu.VMEM((3, 8, 1, 512), F32),
            pltpu.VMEM((4, 8, 32, 512), I16),
            pltpu.VMEM((4, 8, 1, 512), F32),
            pltpu.VMEM((3, 8, 32, 512), I16),
            pltpu.VMEM((3, 8, 1, 512), F32),
            pltpu.VMEM((8, 32, 512), F32),
            pltpu.VMEM((8, 32, 512), F32),
            pltpu.VMEM((4, 2, 32, 512), I16),
            pltpu.VMEM((4, 2, 1, 512), F32),
            pltpu.VMEM((3, 2, 32, 512), I16),
            pltpu.VMEM((3, 2, 1, 512), F32),
            pltpu.VMEM((4, 2, 32, 512), I16),
            pltpu.VMEM((4, 2, 1, 512), F32),
            pltpu.VMEM((3, 2, 32, 512), I16),
            pltpu.VMEM((3, 2, 1, 512), F32),
            pltpu.VMEM((8, 16, 512), F32),
            pltpu.VMEM((8, 16, 512), I16),
            pltpu.VMEM((8, 1, 512), F32),
            pltpu.VMEM((7, 16, 512), I16),
            pltpu.VMEM((7, 1, 512), F32),
            dma((8,)),
            dma((2,)),
            dma((2,)),
            dma((PLANE,)),
            dma((PLANE,)),
            dma((PLANE,)),
            dma((PLANE,)),
            dma((3,)),
            dma((3,)),
            dma((62,)),
            dma((62,)),
        ],
        compiler_params=pltpu.CompilerParams(
            collective_id=1, has_side_effects=True, vmem_limit_bytes=58 << 20
        ),
    )(*operands)


def finish_kernel(end_ref, grads_ref, end_out, grads_out, held, totals, load_sem, store_sem):
    parts = [pl.ds(i * 512, 512) for i in range(4)]
    loads = [pltpu.make_async_copy(end_ref.at[r], held.at[r], load_sem.at[i]) for i, r in enumerate(parts)]
    stores = [pltpu.make_async_copy(held.at[r], end_out.at[r], store_sem.at[i]) for i, r in enumerate(parts)]
    loads.append(pltpu.make_async_copy(grads_ref, totals, load_sem.at[4]))
    stores.append(pltpu.make_async_copy(totals, grads_out, store_sem.at[4]))
    for c in loads:
        c.start()
    for load, store in zip(loads, stores):
        load.wait()
        store.start()
    for c in stores:
        c.wait()


def finish(end, grads):
    hbm = pl.BlockSpec(memory_space=pl.ANY)
    return pl.pallas_call(
        finish_kernel,
        out_shape=[jax.ShapeDtypeStruct(end.shape, end.dtype), jax.ShapeDtypeStruct(grads.shape, grads.dtype)],
        in_specs=[hbm, hbm],
        out_specs=[hbm, hbm],
        scratch_shapes=[
            pltpu.VMEM(end.shape, end.dtype),
            pltpu.VMEM(grads.shape, grads.dtype),
            pltpu.SemaphoreType.DMA((5,)),
            pltpu.SemaphoreType.DMA((5,)),
        ],
        compiler_params=pltpu.CompilerParams(vmem_limit_bytes=58 << 20),
    )(end, grads)


def body(
    head_start,
    flow_start,
    impedance,
    friction,
    seg_count,
    junction_code,
    boundary_code,
    head_up,
    head_down,
    opening,
    window_start,
    layer_weights,
):
    row_total = window_start.shape[0] * lax.axis_size("dp") * 4
    return tuple(
        finish(
            *whole(
            8.0 / row_total,
            head_start,
            flow_start,
            impedance.T,
            friction.T,
            junction_code.T,
            seg_count[None, :],
            boundary_code[None, :],
            head_up[None, :],
            head_down[None, :],
            opening[None, :],
            window_start[None, :],
            layer_weights,
        ))
    )


def solution(mesh):
    placed = (
        P("dp", ("seg", "samp")),
        P("dp", ("seg", "samp")),
        P("dp", None),
        P("dp", None),
        P("dp"),
        P("dp", None),
        P("dp"),
        P("dp"),
        P("dp"),
        P("dp"),
        P("dp"),
        P(),
    )
    return jax.shard_map(
        body,
        mesh=mesh,
        in_specs=placed,
        out_specs=(P("dp", ("seg", "samp")), P(None, ("seg", "samp", "dp"), None)),
        check_vma=False,
    )
```

```python
import functools
import jax
import jax.numpy as jnp
from jax import lax
from jax.experimental import pallas as pl
from jax.experimental.pallas import tpu as pltpu
from jax.sharding import PartitionSpec as P

MESH = pl.DeviceIdType.MESH
PLANE = 32
CELLS = 8192
BF16 = jnp.bfloat16
F32 = jnp.float32
I16 = jnp.int16
TOP = 32767.0
EARLY = 10


def dot(lhs, rhs, lhs_dim, rhs_dim):
    return lax.dot_general(
        lhs, rhs, (((lhs_dim,), (rhs_dim,)), ((), ())), preferred_element_type=F32
    )


def iota(shape, dim):
    return lax.broadcasted_iota(jnp.int32, shape, dim)


def far_first():
    offsets = [(dy, dx, dc) for dy in range(4) for dx in range(4) for dc in range(2)][1:]

    def key(offset):
        dy, dx, dc = offset
        return (min(dy, 4 - dy) + min(dx, 4 - dx), dc, (dx * 7 + dy * 3) % 5)

    return sorted(offsets, key=key, reverse=True)


def eye(size):
    return jnp.where(iota((size, size), 0) == iota((size, size), 1), 1.0, 0.0).astype(BF16)


W_LO, W_HI, L_LO, L_HI, H_LO, H_HI, FIRST, COUNT, END_A, END_L, END_Q, UPPER = range(12)


def prepare_params(position, imp_ref, fric_ref, junc_ref, count_ref, kind_ref, up_ref, down_ref, open_ref, prm):
    wide = imp_ref.shape
    imp = imp_ref[...]
    loss = fric_ref[...] * (1.0 + junc_ref[...].astype(F32))
    count = count_ref[...]
    before = position * 256 - 1
    section = lax.shift_right_logical(jnp.maximum(before, 0) * count, 13)
    row = iota(wide, 0)

    def pick(values, number):
        return jnp.sum(jnp.where(row == number, values, 0.0), axis=0, keepdims=True)

    w_lo, w_hi = pick(imp, section), pick(imp, section + 1)
    w_end = pick(imp, count - 1)
    prm[W_LO : W_LO + 1] = w_lo
    prm[W_HI : W_HI + 1] = w_hi
    prm[L_LO : L_LO + 1] = pick(loss, section)
    prm[L_HI : L_HI + 1] = pick(loss, section + 1)
    prm[H_LO : H_LO + 1] = 0.5 / w_lo
    prm[H_HI : H_HI + 1] = 0.5 / jnp.where(w_hi == 0.0, 1.0, w_hi)
    prm[FIRST : FIRST + 1] = (before * count - (section + 1) * CELLS).astype(F32)
    prm[COUNT : COUNT + 1] = count.astype(F32)
    kind, valve = kind_ref[...], open_ref[...]
    factor = 1.0 / (1.0 + w_end * valve)
    prm[END_A : END_A + 1] = jnp.where(kind == 0, 0.0, jnp.where(kind == 1, 1.0, factor))
    prm[END_L : END_L + 1] = jnp.where(kind == 0, down_ref[...], 0.0)
    prm[END_Q : END_Q + 1] = jnp.where(kind == 0, 1.0 / w_end, jnp.where(kind == 1, 0.0, valve * factor))
    prm[UPPER : UPPER + 1] = up_ref[...]


def stencil_tile(position, tile, prm, heads, flows, h1, q1, turned):
    lanes = pl.ds(pl.multiple_of(tile * 128, 128), 128)

    def param(number, rows=8):
        return jnp.broadcast_to(prm[number : number + 1, lanes], (rows, 128))

    count = param(COUNT)
    start = param(FIRST) + iota((8, 128), 0).astype(F32) * count
    lows = [param(W_LO), param(L_LO), param(H_LO)]
    highs = [param(W_HI), param(L_HI), param(H_HI)]

    def fields(value, number):
        high = value >= 0.0
        return [jnp.where(high, highs[k], lows[k]) for k in range(number)]

    def ends(lh, lq, rh, rq, wave, loss):
        forward = lh + lq * (wave - loss * jnp.abs(lq))
        backward = rh - rq * (wave - loss * jnp.abs(rq))
        return forward, backward

    def first(g, value):
        wave, loss, half = fields(value, 3)
        left, right = pl.ds(8 * g + 6, 8), pl.ds(8 * g + 8, 8)
        forward, backward = ends(
            heads[tile, left, :], flows[tile, left, :], heads[tile, right, :], flows[tile, right, :], wave, loss
        )
        return forward, backward, half

    value = start
    for g in range(33):
        forward, backward, half = first(g, value)
        h1[8 * g : 8 * g + 8] = 0.5 * (forward + backward)
        q1[8 * g : 8 * g + 8] = (forward - backward) * half
        value = value + 8.0 * count

    @pl.when(position == 0)
    def _():
        _, backward, half = first(0, start)
        upper = param(UPPER)
        at = iota((8, 128), 0) == 1
        h1[0:8] = jnp.where(at, upper, h1[0:8])
        q1[0:8] = jnp.where(at, (upper - backward) * (2.0 * half), q1[0:8])

    @pl.when(position == PLANE - 1)
    def _():
        forward, _, _ = first(32, start + 256.0 * count)
        at = iota((8, 128), 0) == 0
        h1[256:264] = jnp.where(at, param(END_A) * forward + param(END_L), h1[256:264])
        q1[256:264] = jnp.where(at, (forward - param(END_L)) * param(END_Q), q1[256:264])

    def second(g, value):
        wave, loss = fields(value, 2)
        left, right = pl.ds(8 * g, 8), pl.ds(8 * g + 2, 8)
        return ends(h1[left, :], q1[left, :], h1[right, :], q1[right, :], wave, loss)

    value = start + count
    for g in range(16):
        pieces = []
        for _ in range(2):
            forward, backward = second(2 * g + len(pieces), value)
            pieces.append(0.5 * (forward + backward))
            value = value + 8.0 * count
        turned[16 * g : 16 * g + 16] = jnp.concatenate(pieces, axis=0).astype(BF16)

    @pl.when(position == 0)
    def _():
        at = iota((16, 128), 0) == 0
        turned[0:16] = jnp.where(at, param(UPPER, 16), turned[0:16].astype(F32)).astype(BF16)

    @pl.when(position == PLANE - 1)
    def _():
        forward, _ = second(31, start + 249.0 * count)
        last = param(END_A) * forward + param(END_L)
        last = jnp.concatenate([last, last], axis=0)
        at = iota((16, 128), 0) == 15
        turned[240:256] = jnp.where(at, last, turned[240:256].astype(F32)).astype(BF16)


def cut_windows(rows_ref, begin_ref, out_ref):
    def group(number, carry):
        here = pl.ds(pl.multiple_of(number * 16, 16), 16)
        begin = begin_ref[here, :]
        block = lax.shift_right_logical(begin, 7).astype(I16)
        rest = begin & 127
        lane = iota((16, 128), 1)
        values = []
        for source in range(PLANE):
            pair = rows_ref[source, here, :]
            values += [pair[:, :128], pair[:, 128:]]
        for bit, count in ((32, 64), (16, 48), (8, 40), (4, 36), (2, 34), (1, 33)):
            on = (block & jnp.int16(bit)) != 0
            values = [
                jnp.where(on, values[j + bit], values[j]) if j + bit < len(values) else values[j]
                for j in range(count)
            ]
        index = (lane + rest) & 127
        keep = lane + rest < 128
        moved = [jnp.take_along_axis(v.astype(F32), index, axis=1) for v in values]
        for j in range(32):
            piece = jnp.where(keep, moved[j], moved[j + 1]).astype(BF16)
            at = pl.ds(pl.multiple_of((j // 8) * 64 + number * 16, 16), 16)
            out_ref[at, (j % 8) * 128 : (j % 8) * 128 + 128] = piece
        return carry

    lax.fori_loop(0, 4, group, 0)


def coded(block):
    top = jnp.maximum(jnp.max(jnp.abs(block), axis=0, keepdims=True), 1e-30)
    return jnp.round(block * (TOP / top)).astype(I16), top * (1.0 / TOP)


def decoded(number_ref, scale_ref, index):
    return number_ref[index].astype(F32) * scale_ref[index]


def kernel(
    scale,
    head_hbm, flow_hbm, imp_hbm, fric_hbm, junc_hbm, count_hbm, kind_hbm, up_hbm, down_hbm, open_hbm, begin_hbm,
    weights_hbm,
    end_ref, grads_ref,
    imp_ref, fric_ref, junc_ref, count_ref, kind_ref, up_ref, down_ref, open_ref, begin_ref,
    head, flow, weights, prm, halo_out, halo_in, heads, flows, h1, q1, turned, head_end,
    start_rows, end_rows, begin, a0, a1, z_val, out_val, targets, at_own, at_in, g_own, g_in,
    d_sum, sf, sfs, rf, rfs, sn, sns, rn, rns, a_sum, b_sum, sa2, sa2s, ra2, ra2s, sb2, sb2s, rb2, rb2s,
    z_sum, sz, szs, rz, rzs,
    lsem, halo_sem, old_sem, new_sem, csend, crecv, relay_sem, first_sem, early_send, second_sem, third_sem,
):
    seg, samp, zpos = lax.axis_index("seg"), lax.axis_index("samp"), lax.axis_index("dp")
    y, xlo, core = seg // 4, (seg // 2) % 2, seg % 2
    x = samp * 2 + xlo
    position = seg * 2 + samp

    def at_plane(t):
        return {"seg": t // 2, "samp": t % 2}

    def neighbour(offset):
        tx = (x + offset[1]) % 4
        return ((y + offset[0]) % 4) * 8 + (tx % 2) * 4 + ((core + offset[2]) % 2) * 2 + tx // 2

    def at_x(t):
        return {"seg": y * 4 + (t % 2) * 2 + core, "samp": t // 2}

    def at_y(t):
        return {"seg": t * 4 + xlo * 2 + core}

    def at_z(t):
        return {"dp": t}

    at_core = {"seg": y * 4 + xlo * 2 + 1 - core}

    def remote(src, dst, send, recv, device):
        return pltpu.make_async_remote_copy(
            src_ref=src, dst_ref=dst, send_sem=send, recv_sem=recv, device_id=device, device_id_type=MESH
        )

    def take(ref, sem):
        pltpu.make_async_copy(ref, ref, sem).wait()

    barrier = pltpu.get_barrier_semaphore()

    for p in (4, 3, 5, 2, 6, 1, 7):
        pl.semaphore_signal(barrier, inc=1, device_id=at_z((zpos + p) % 8), device_id_type=MESH)
    for offset in far_first():
        pl.semaphore_signal(barrier, inc=1, device_id=at_plane(neighbour(offset)), device_id_type=MESH)

    loads = [
        pltpu.make_async_copy(source, target, lsem.at[3 + number])
        for number, (source, target) in enumerate(
            (
                (head_hbm, head), (flow_hbm, flow), (imp_hbm, imp_ref), (fric_hbm, fric_ref), (junc_hbm, junc_ref),
                (count_hbm, count_ref), (kind_hbm, kind_ref), (up_hbm, up_ref), (down_hbm, down_ref),
                (open_hbm, open_ref), (begin_hbm, begin_ref), (weights_hbm, weights),
            )
        )
    ]
    for c in loads[:11]:
        c.start()

    pl.semaphore_wait(barrier, 38)

    def block(t):
        return pl.ds(pl.multiple_of(t * 64, 64), 64)

    def spread(source, target, sem, t):
        return remote(source.at[block(t)], target.at[position], sem.at[0], sem.at[1], at_plane(t))

    def send_old(offset):
        spread(head_hbm, start_rows, old_sem, neighbour(offset)).start()

    for offset in far_first()[:EARLY]:
        send_old(offset)

    row, lane = iota((16, 256), 0), iota((16, 256), 1)
    pick = jnp.where((row < 4) & (lane == jnp.where(row < 2, row, row + 252)), 1.0, 0.0).astype(BF16)
    halo_out[...] = jnp.zeros_like(halo_out)
    loads[0].wait()
    edge = dot(pick, head[...], 1, 1)
    halo_out[0, 0:2] = edge[0:2]
    halo_out[1, 0:2] = edge[2:4]
    loads[1].wait()
    edge = dot(pick, flow[...], 1, 1)
    halo_out[0, 2:4] = edge[0:2]
    halo_out[1, 2:4] = edge[2:4]

    below, above = (position + PLANE - 1) % PLANE, (position + 1) % PLANE
    halos = [
        remote(halo_out.at[0], halo_in.at[0], halo_sem.at[0], halo_sem.at[1], at_plane(below)),
        remote(halo_out.at[1], halo_in.at[1], halo_sem.at[0], halo_sem.at[1], at_plane(above)),
    ]
    for c in halos:
        c.start()

    for offset in far_first()[EARLY:]:
        send_old(offset)
    loads[11].start()
    keep_old = pltpu.make_async_copy(head.at[block(position)], start_rows.at[position], lsem.at[0])
    keep_old.start()

    for c in loads[2:11]:
        c.wait()
    prepare_params(position, imp_ref, fric_ref, junc_ref, count_ref, kind_ref, up_ref, down_ref, open_ref, prm)
    lanes = pl.ds(pl.multiple_of((position // 2) * 128, 128), 128)
    own_begin = jnp.broadcast_to(begin_ref[:, lanes].astype(F32), (64, 128))
    chosen = iota((64, 128), 1) == iota((64, 128), 0) + (position % 2) * 64
    own_begin = jnp.sum(jnp.where(chosen, own_begin, 0.0), axis=1, keepdims=True)
    begin[...] = jnp.broadcast_to(own_begin, (64, 128)).astype(jnp.int32)
    unit = eye(256)

    def turn(t, c):
        rows = pl.ds(pl.multiple_of(t * 128, 128), 128)
        heads[t, 8:264, :] = dot(unit, head[rows, :], 1, 1)
        flows[t, 8:264, :] = dot(unit, flow[rows, :], 1, 1)
        return c

    lax.fori_loop(0, 16, turn, 0)
    take(halo_in, halo_sem.at[1])

    small = eye(128)

    def one_tile(i, c):
        turn_y = i // 4
        turn_y = jnp.where(turn_y < 2, 2 - turn_y, 6 - turn_y)
        turn_y = jnp.where(i >= 12, 0, jnp.where(i >= 8, 3, turn_y))
        tile = ((y + turn_y) % 4) * 4 + (xlo * 2 + core + i) % 4
        lanes = pl.ds(pl.multiple_of(tile * 128, 128), 128)
        heads[tile, 264:266, :] = halo_in[0, 0:2, lanes]
        flows[tile, 264:266, :] = halo_in[0, 2:4, lanes]
        heads[tile, 6:8, :] = halo_in[1, 0:2, lanes]
        flows[tile, 6:8, :] = halo_in[1, 2:4, lanes]
        stencil_tile(position, tile, prm, heads, flows, h1, q1, turned)
        head_end[pl.ds(pl.multiple_of(tile * 128, 128), 128), :] = dot(small, turned[...], 1, 1).astype(BF16)
        for k in range(2):
            t = 2 * tile + k

            @pl.when(t != position)
            def _():
                spread(head_end, end_rows, new_sem, t).start()

        return c

    lax.fori_loop(0, 16, one_tile, 0)
    keep_new = pltpu.make_async_copy(head_end.at[block(position)], end_rows.at[position], lsem.at[1])
    keep_new.start()
    store_end = pltpu.make_async_copy(head_end, end_ref, lsem.at[2])
    store_end.start()

    loads[11].wait()
    keep_old.wait()

    take(start_rows.at[pl.ds(0, PLANE - 1)], old_sem.at[1])
    cut_windows(start_rows, begin, a0)
    for c in range(4):
        cols = slice(c * 256, c * 256 + 256)
        z = dot(a0[...], weights[0, :, cols], 1, 0)
        z_val[:, cols] = z
        a1[:, cols] = (z * jax.nn.sigmoid(z)).astype(BF16)
    for c in range(4):
        cols = slice(c * 256, c * 256 + 256)
        out_val[:, cols] = dot(a1[...], weights[1, :, cols], 1, 0)

    def turn_a(b, c):
        cols = pl.ds(pl.multiple_of(b * 128, 128), 128)
        for layer, source in ((0, a0), (1, a1)):
            both = source[:, cols].T
            at_own[layer, 0, b] = both[0:64]
            at_own[layer, 1, b] = both[64:128]
        return c

    lax.fori_loop(0, 8, turn_a, 0)
    core_a = remote(at_own.at[:, 1 - core], at_in, csend.at[0], crecv.at[0], at_core)
    core_a.start()

    keep_new.wait()

    take(end_rows.at[pl.ds(0, PLANE - 1)], new_sem.at[1])
    cut_windows(end_rows, begin, targets)
    g_own[1] = ((out_val[...] - targets[...].astype(F32)) * scale).astype(BF16)
    core_g1 = remote(g_own.at[1], g_in.at[1], csend.at[1], crecv.at[1], at_core)
    core_g1.start()
    for c in range(4):
        cols = slice(c * 256, c * 256 + 256)
        back = dot(g_own[1], weights[1, cols, :], 1, 1)
        z = z_val[:, cols]
        sigma = jax.nn.sigmoid(z)
        g_own[0, :, cols] = (back * sigma * (1.0 + z * (1.0 - sigma))).astype(BF16)
    core_g0 = remote(g_own.at[0], g_in.at[0], csend.at[2], crecv.at[2], at_core)
    core_g0.start()

    def share(layer, side, target, i):
        if side == 0:
            return d_sum[layer * 8 + i * 2 + target % 2, pl.ds(pl.multiple_of((target // 2) * 32, 32), 32), 0:512]
        return d_sum[layer * 8 + target * 2 + i % 2, pl.ds(pl.multiple_of((i // 2) * 32, 32), 32), 512:1024]

    def way(layer, side, step, source, target, first, forth):
        here, at = (x, at_x) if side == 0 else (y, at_y)
        device = at((here + (1 if forth else 3)) % 4)
        part = pl.ds(first, 2)
        lane = 0 if forth else 1
        sem = relay_sem if step == 0 else first_sem
        for k in range(2):
            remote(
                source[k].at[side, lane, part],
                target[k].at[side, lane, part],
                early_send.at[k if step == 0 else 2 + k],
                sem.at[layer, side, k],
                device,
            ).start()

    def begin_exchange(layer, side):
        here = x if side == 0 else y
        base = layer * 4

        def far(i, c):
            numbers, scales = coded(share(layer, side, (here + 2) % 4, i))
            lane = i // 2
            sf[side, lane, base + i], sfs[side, lane, base + i] = numbers, scales
            return c

        lax.fori_loop(0, 4, far, 0)
        way(layer, side, 0, (sf, sfs), (rf, rfs), base, True)
        way(layer, side, 0, (sf, sfs), (rf, rfs), base + 2, False)

        def near(i, c):
            sn[side, 0, base + 2 + i], sns[side, 0, base + 2 + i] = coded(share(layer, side, (here + 1) % 4, 2 + i))
            sn[side, 1, base + i], sns[side, 1, base + i] = coded(share(layer, side, (here + 3) % 4, i))
            return c

        lax.fori_loop(0, 2, near, 0)
        way(layer, side, 1, (sn, sns), (rn, rns), base + 2, True)
        way(layer, side, 1, (sn, sns), (rn, rns), base, False)

    def pass_on(layer, side):
        here = x if side == 0 else y
        base = layer * 4
        take(rf.at[side, :, pl.ds(base, 2)], relay_sem.at[layer, side, 0])
        take(rfs.at[side, :, pl.ds(base, 2)], relay_sem.at[layer, side, 1])

        def add(i, c):
            at = base + i
            up = share(layer, side, (here + 1) % 4, i) + rf[side, 0, at].astype(F32) * rfs[side, 0, at]
            sn[side, 0, at], sns[side, 0, at] = coded(up)
            at = base + 2 + i
            down = share(layer, side, (here + 3) % 4, 2 + i) + rf[side, 1, at].astype(F32) * rfs[side, 1, at]
            sn[side, 1, at], sns[side, 1, at] = coded(down)
            return c

        lax.fori_loop(0, 2, add, 0)
        way(layer, side, 2, (sn, sns), (rn, rns), base, True)
        way(layer, side, 2, (sn, sns), (rn, rns), base + 2, False)

    def product(layer, c, left, right):
        cols = slice(c * 256, c * 256 + 256)
        return dot(left.reshape(512, 256), right[layer, :, cols], 1, 0).reshape(8, 64, 256)

    def own_product(layer):
        for c in range(4):
            d_sum[layer * 8 : layer * 8 + 8, :, c * 256 : c * 256 + 256] = product(
                layer, c, at_own[layer, core], g_own
            )

    def add_product(layer, side):
        for c in (2 * side, 2 * side + 1):
            d_sum[layer * 8 : layer * 8 + 8, :, c * 256 : c * 256 + 256] += product(layer, c, at_in[layer], g_in)

    core_a.wait_recv()
    own_product(1)
    core_g1.wait_recv()
    add_product(1, 0)
    begin_exchange(1, 0)
    add_product(1, 1)
    begin_exchange(1, 1)
    own_product(0)
    core_g0.wait_recv()
    add_product(0, 0)
    begin_exchange(0, 0)
    pass_on(1, 0)
    add_product(0, 1)
    begin_exchange(0, 1)
    pass_on(1, 1)
    pass_on(0, 0)
    pass_on(0, 1)

    for layer in (1, 0):
        for side in range(2):
            take(rn.at[side, :, pl.ds(layer * 4, 4)], first_sem.at[layer, side, 0])
            take(rns.at[side, :, pl.ds(layer * 4, 4)], first_sem.at[layer, side, 1])

            def add_up(i, c, layer=layer, side=side):
                at = layer * 4 + i
                total = share(layer, side, y if side else x, i)
                for lane in range(2):
                    total = total + rn[side, lane, at].astype(F32) * rns[side, lane, at]
                if side == 0:
                    a_sum[at] = total
                    sa2[i, layer], sa2s[i, layer] = coded(total)
                else:
                    b_sum[at] = total
                    sb2[i, layer], sb2s[i, layer] = coded(total)
                return c

            lax.fori_loop(0, 4, add_up, 0)
            for p in (2, 1, 3):
                tx, ty = (x + p) % 4, (y + p) % 4
                parts = (
                    ((sa2, ra2, ty, at_y(ty)), (sa2s, ra2s, ty, at_y(ty)))
                    if side == 0
                    else ((sb2, rb2, tx, at_x(tx)), (sb2s, rb2s, tx, at_x(tx)))
                )
                for k, (source, target, t, device) in enumerate(parts):
                    k = 2 * side + k
                    remote(
                        source.at[t, layer], target.at[p - 1, layer], second_sem.at[0, k], second_sem.at[1, k], device
                    ).start()
    for k, ref in enumerate((ra2, ra2s, rb2, rb2s)):
        take(ref, second_sem.at[1, k])

    for layer in range(2):
        left = a_sum[layer * 4 + y]
        right = b_sum[layer * 4 + x]
        for p in range(3):
            left = left + ra2[p, layer].astype(F32) * ra2s[p, layer]
            right = right + rb2[p, layer].astype(F32) * rb2s[p, layer]
        for t in range(8):
            z_sum[t, 4 * layer : 4 * layer + 4] = left[4 * t : 4 * t + 4]
            z_sum[t, 8 + 4 * layer : 12 + 4 * layer] = right[4 * t : 4 * t + 4]
    for t in range(8):
        sz[t], szs[t] = coded(z_sum[t])
    for p in (4, 3, 5, 2, 6, 1, 7):
        t = (zpos + p) % 8
        remote(sz.at[t], rz.at[p - 1], third_sem.at[0, 0], third_sem.at[1, 0], at_z(t)).start()
        remote(szs.at[t], rzs.at[p - 1], third_sem.at[0, 1], third_sem.at[1, 1], at_z(t)).start()
    take(rz, third_sem.at[1, 0])
    take(rzs, third_sem.at[1, 1])
    total = z_sum[zpos]
    for p in range(7):
        total = total + rz[p].astype(F32) * rzs[p]
    for layer in range(2):
        grads_ref[layer, :, 0:512] = total[4 * layer : 4 * layer + 4]
        grads_ref[layer, :, 512:1024] = total[8 + 4 * layer : 12 + 4 * layer]
    take(halo_out, halo_sem.at[0])
    take(start_rows.at[pl.ds(0, PLANE - 1)], old_sem.at[0])
    take(end_rows.at[pl.ds(0, PLANE - 1)], new_sem.at[0])
    core_a.wait_send()
    core_g1.wait_send()
    core_g0.wait_send()
    for k, ref in enumerate((sf.at[0], sfs.at[0], sn, sns)):
        take(ref, early_send.at[k])
    for k, ref in enumerate((ra2, ra2s, rb2, rb2s)):
        take(ref, second_sem.at[0, k])
    take(rz, third_sem.at[0, 0])
    take(rzs, third_sem.at[0, 1])
    store_end.wait()


def whole(scale, *operands):
    hbm = pl.BlockSpec(memory_space=pl.ANY)
    vmem = pl.BlockSpec(memory_space=pltpu.VMEM)
    dma = pltpu.SemaphoreType.DMA
    return pl.pallas_call(
        functools.partial(kernel, scale),
        out_shape=[
            jax.ShapeDtypeStruct((2048, 256), BF16),
            jax.ShapeDtypeStruct((2, 4, 1024), F32),
        ],
        in_specs=[hbm] * 12,
        out_specs=[hbm, vmem],
        scratch_shapes=[
            pltpu.VMEM((8, 2048), F32),
            pltpu.VMEM((8, 2048), F32),
            pltpu.VMEM((8, 2048), jnp.int32),
            pltpu.VMEM((1, 2048), jnp.int32),
            pltpu.VMEM((1, 2048), jnp.int32),
            pltpu.VMEM((1, 2048), F32),
            pltpu.VMEM((1, 2048), F32),
            pltpu.VMEM((1, 2048), F32),
            pltpu.VMEM((1, 2048), jnp.int32),
            pltpu.VMEM((2048, 256), BF16),
            pltpu.VMEM((2048, 256), BF16),
            pltpu.VMEM((2, 1024, 1024), BF16),
            pltpu.VMEM((16, 2048), F32),
            pltpu.VMEM((2, 8, 2048), F32),
            pltpu.VMEM((2, 8, 2048), F32),
            pltpu.VMEM((16, 272, 128), F32),
            pltpu.VMEM((16, 272, 128), F32),
            pltpu.VMEM((264, 128), F32),
            pltpu.VMEM((264, 128), F32),
            pltpu.VMEM((256, 128), BF16),
            pltpu.VMEM((2048, 256), BF16),
            pltpu.VMEM((32, 64, 256), BF16),
            pltpu.VMEM((32, 64, 256), BF16),
            pltpu.VMEM((64, 128), jnp.int32),
            pltpu.VMEM((256, 1024), BF16),
            pltpu.VMEM((256, 1024), BF16),
            pltpu.VMEM((256, 1024), F32),
            pltpu.VMEM((256, 1024), F32),
            pltpu.VMEM((256, 1024), BF16),
            pltpu.VMEM((2, 2, 8, 64, 256), BF16),
            pltpu.VMEM((2, 8, 64, 256), BF16),
            pltpu.VMEM((2, 256, 1024), BF16),
            pltpu.VMEM((2, 256, 1024), BF16),
            pltpu.VMEM((16, 64, 1024), F32),
            pltpu.VMEM((2, 2, 8, 32, 512), I16),
            pltpu.VMEM((2, 2, 8, 1, 512), F32),
            pltpu.VMEM((2, 2, 8, 32, 512), I16),
            pltpu.VMEM((2, 2, 8, 1, 512), F32),
            pltpu.VMEM((2, 2, 8, 32, 512), I16),
            pltpu.VMEM((2, 2, 8, 1, 512), F32),
            pltpu.VMEM((2, 2, 8, 32, 512), I16),
            pltpu.VMEM((2, 2, 8, 1, 512), F32),
            pltpu.VMEM((8, 32, 512), F32),
            pltpu.VMEM((8, 32, 512), F32),
            pltpu.VMEM((4, 2, 32, 512), I16),
            pltpu.VMEM((4, 2, 1, 512), F32),
            pltpu.VMEM((3, 2, 32, 512), I16),
            pltpu.VMEM((3, 2, 1, 512), F32),
            pltpu.VMEM((4, 2, 32, 512), I16),
            pltpu.VMEM((4, 2, 1, 512), F32),
            pltpu.VMEM((3, 2, 32, 512), I16),
            pltpu.VMEM((3, 2, 1, 512), F32),
            pltpu.VMEM((8, 16, 512), F32),
            pltpu.VMEM((8, 16, 512), I16),
            pltpu.VMEM((8, 1, 512), F32),
            pltpu.VMEM((7, 16, 512), I16),
            pltpu.VMEM((7, 1, 512), F32),
            dma((15,)),
            dma((2,)),
            dma((2,)),
            dma((2,)),
            dma((3,)),
            dma((3,)),
            dma((2, 2, 2)),
            dma((2, 2, 2)),
            dma((4,)),
            dma((2, 4)),
            dma((2, 2)),
        ],
        compiler_params=pltpu.CompilerParams(
            collective_id=1, has_side_effects=True, vmem_limit_bytes=58 << 20
        ),
    )(*operands)


def finish_kernel(end_ref, grads_ref, end_out, grads_out, held, totals, load_sem, store_sem):
    parts = [pl.ds(i * 512, 512) for i in range(4)]
    loads = [pltpu.make_async_copy(end_ref.at[r], held.at[r], load_sem.at[i]) for i, r in enumerate(parts)]
    stores = [pltpu.make_async_copy(held.at[r], end_out.at[r], store_sem.at[i]) for i, r in enumerate(parts)]
    loads.append(pltpu.make_async_copy(grads_ref, totals, load_sem.at[4]))
    stores.append(pltpu.make_async_copy(totals, grads_out, store_sem.at[4]))
    for c in loads:
        c.start()
    for load, store in zip(loads, stores):
        load.wait()
        store.start()
    for c in stores:
        c.wait()


def finish(end, grads):
    hbm = pl.BlockSpec(memory_space=pl.ANY)
    return pl.pallas_call(
        finish_kernel,
        out_shape=[jax.ShapeDtypeStruct(end.shape, end.dtype), jax.ShapeDtypeStruct(grads.shape, grads.dtype)],
        in_specs=[hbm, hbm],
        out_specs=[hbm, hbm],
        scratch_shapes=[
            pltpu.VMEM(end.shape, end.dtype),
            pltpu.VMEM(grads.shape, grads.dtype),
            pltpu.SemaphoreType.DMA((5,)),
            pltpu.SemaphoreType.DMA((5,)),
        ],
        compiler_params=pltpu.CompilerParams(vmem_limit_bytes=58 << 20),
    )(end, grads)


def body(
    head_start,
    flow_start,
    impedance,
    friction,
    seg_count,
    junction_code,
    boundary_code,
    head_up,
    head_down,
    opening,
    window_start,
    layer_weights,
):
    row_total = window_start.shape[0] * lax.axis_size("dp") * 4
    return tuple(
        finish(
            *whole(
            8.0 / row_total,
            head_start,
            flow_start,
            impedance.T,
            friction.T,
            junction_code.T,
            seg_count[None, :],
            boundary_code[None, :],
            head_up[None, :],
            head_down[None, :],
            opening[None, :],
            window_start[None, :],
            layer_weights,
        ))
    )


def solution(mesh):
    placed = (
        P("dp", ("seg", "samp")),
        P("dp", ("seg", "samp")),
        P("dp", None),
        P("dp", None),
        P("dp"),
        P("dp", None),
        P("dp"),
        P("dp"),
        P("dp"),
        P("dp"),
        P("dp"),
        P(),
    )
    return jax.shard_map(
        body,
        mesh=mesh,
        in_specs=placed,
        out_specs=(P("dp", ("seg", "samp")), P(None, ("seg", "samp", "dp"), None)),
        check_vma=False,
    )
```

```python
import functools
import jax
import jax.numpy as jnp
from jax import lax
from jax.experimental import pallas as pl
from jax.experimental.pallas import tpu as pltpu
from jax.sharding import PartitionSpec as P

MESH = pl.DeviceIdType.MESH
PLANE = 32
CELLS = 8192
BF16 = jnp.bfloat16
F32 = jnp.float32
I16 = jnp.int16
TOP = 32767.0
EARLY = 10


def dot(lhs, rhs, lhs_dim, rhs_dim):
    return lax.dot_general(
        lhs, rhs, (((lhs_dim,), (rhs_dim,)), ((), ())), preferred_element_type=F32
    )


def iota(shape, dim):
    return lax.broadcasted_iota(jnp.int32, shape, dim)


def far_first():
    offsets = [(dy, dx, dc) for dy in range(4) for dx in range(4) for dc in range(2)][1:]

    def key(offset):
        dy, dx, dc = offset
        return (min(dy, 4 - dy) + min(dx, 4 - dx), dc, (dx * 7 + dy * 3) % 5)

    return sorted(offsets, key=key, reverse=True)


def eye(size):
    return jnp.where(iota((size, size), 0) == iota((size, size), 1), 1.0, 0.0).astype(BF16)


W_LO, W_HI, L_LO, L_HI, H_LO, H_HI, FIRST, COUNT, END_A, END_L, END_Q, UPPER = range(12)


def prepare_params(position, imp_ref, fric_ref, junc_ref, count_ref, kind_ref, up_ref, down_ref, open_ref, prm):
    wide = imp_ref.shape
    imp = imp_ref[...]
    loss = fric_ref[...] * (1.0 + junc_ref[...].astype(F32))
    count = count_ref[...]
    before = position * 256 - 1
    section = lax.shift_right_logical(jnp.maximum(before, 0) * count, 13)
    row = iota(wide, 0)

    def pick(values, number):
        return jnp.sum(jnp.where(row == number, values, 0.0), axis=0, keepdims=True)

    w_lo, w_hi = pick(imp, section), pick(imp, section + 1)
    w_end = pick(imp, count - 1)
    prm[W_LO : W_LO + 1] = w_lo
    prm[W_HI : W_HI + 1] = w_hi
    prm[L_LO : L_LO + 1] = pick(loss, section)
    prm[L_HI : L_HI + 1] = pick(loss, section + 1)
    prm[H_LO : H_LO + 1] = 0.5 / w_lo
    prm[H_HI : H_HI + 1] = 0.5 / jnp.where(w_hi == 0.0, 1.0, w_hi)
    prm[FIRST : FIRST + 1] = (before * count - (section + 1) * CELLS).astype(F32)
    prm[COUNT : COUNT + 1] = count.astype(F32)
    kind, valve = kind_ref[...], open_ref[...]
    factor = 1.0 / (1.0 + w_end * valve)
    prm[END_A : END_A + 1] = jnp.where(kind == 0, 0.0, jnp.where(kind == 1, 1.0, factor))
    prm[END_L : END_L + 1] = jnp.where(kind == 0, down_ref[...], 0.0)
    prm[END_Q : END_Q + 1] = jnp.where(kind == 0, 1.0 / w_end, jnp.where(kind == 1, 0.0, valve * factor))
    prm[UPPER : UPPER + 1] = up_ref[...]


def stencil_tile(position, tile, prm, heads, flows, h1, q1, turned):
    lanes = pl.ds(pl.multiple_of(tile * 128, 128), 128)

    def param(number, rows=8):
        return jnp.broadcast_to(prm[number : number + 1, lanes], (rows, 128))

    count = param(COUNT)
    start = param(FIRST) + iota((8, 128), 0).astype(F32) * count
    lows = [param(W_LO), param(L_LO), param(H_LO)]
    highs = [param(W_HI), param(L_HI), param(H_HI)]

    def fields(value, number):
        high = value >= 0.0
        return [jnp.where(high, highs[k], lows[k]) for k in range(number)]

    def ends(lh, lq, rh, rq, wave, loss):
        forward = lh + lq * (wave - loss * jnp.abs(lq))
        backward = rh - rq * (wave - loss * jnp.abs(rq))
        return forward, backward

    def first(g, value):
        wave, loss, half = fields(value, 3)
        left, right = pl.ds(8 * g + 6, 8), pl.ds(8 * g + 8, 8)
        forward, backward = ends(
            heads[tile, left, :], flows[tile, left, :], heads[tile, right, :], flows[tile, right, :], wave, loss
        )
        return forward, backward, half

    value = start
    for g in range(33):
        forward, backward, half = first(g, value)
        h1[8 * g : 8 * g + 8] = 0.5 * (forward + backward)
        q1[8 * g : 8 * g + 8] = (forward - backward) * half
        value = value + 8.0 * count

    @pl.when(position == 0)
    def _():
        _, backward, half = first(0, start)
        upper = param(UPPER)
        at = iota((8, 128), 0) == 1
        h1[0:8] = jnp.where(at, upper, h1[0:8])
        q1[0:8] = jnp.where(at, (upper - backward) * (2.0 * half), q1[0:8])

    @pl.when(position == PLANE - 1)
    def _():
        forward, _, _ = first(32, start + 256.0 * count)
        at = iota((8, 128), 0) == 0
        h1[256:264] = jnp.where(at, param(END_A) * forward + param(END_L), h1[256:264])
        q1[256:264] = jnp.where(at, (forward - param(END_L)) * param(END_Q), q1[256:264])

    def second(g, value):
        wave, loss = fields(value, 2)
        left, right = pl.ds(8 * g, 8), pl.ds(8 * g + 2, 8)
        return ends(h1[left, :], q1[left, :], h1[right, :], q1[right, :], wave, loss)

    value = start + count
    for g in range(16):
        pieces = []
        for _ in range(2):
            forward, backward = second(2 * g + len(pieces), value)
            pieces.append(0.5 * (forward + backward))
            value = value + 8.0 * count
        turned[16 * g : 16 * g + 16] = jnp.concatenate(pieces, axis=0).astype(BF16)

    @pl.when(position == 0)
    def _():
        at = iota((16, 128), 0) == 0
        turned[0:16] = jnp.where(at, param(UPPER, 16), turned[0:16].astype(F32)).astype(BF16)

    @pl.when(position == PLANE - 1)
    def _():
        forward, _ = second(31, start + 249.0 * count)
        last = param(END_A) * forward + param(END_L)
        last = jnp.concatenate([last, last], axis=0)
        at = iota((16, 128), 0) == 15
        turned[240:256] = jnp.where(at, last, turned[240:256].astype(F32)).astype(BF16)


def cut_windows(rows_ref, begin_ref, out_ref):
    def group(number, carry):
        here = pl.ds(pl.multiple_of(number * 16, 16), 16)
        begin = begin_ref[here, :]
        block = lax.shift_right_logical(begin, 7).astype(I16)
        rest = begin & 127
        lane = iota((16, 128), 1)
        values = []
        for source in range(PLANE):
            pair = rows_ref[source, here, :]
            values += [pair[:, :128], pair[:, 128:]]
        for bit, count in ((32, 64), (16, 48), (8, 40), (4, 36), (2, 34), (1, 33)):
            on = (block & jnp.int16(bit)) != 0
            values = [
                jnp.where(on, values[j + bit], values[j]) if j + bit < len(values) else values[j]
                for j in range(count)
            ]
        index = (lane + rest) & 127
        keep = lane + rest < 128
        moved = [jnp.take_along_axis(v.astype(F32), index, axis=1) for v in values]
        for j in range(32):
            piece = jnp.where(keep, moved[j], moved[j + 1]).astype(BF16)
            at = pl.ds(pl.multiple_of((j // 8) * 64 + number * 16, 16), 16)
            out_ref[at, (j % 8) * 128 : (j % 8) * 128 + 128] = piece
        return carry

    lax.fori_loop(0, 4, group, 0)


def coded(block):
    top = jnp.maximum(jnp.max(jnp.abs(block), axis=0, keepdims=True), 1e-30)
    return jnp.round(block * (TOP / top)).astype(I16), top * (1.0 / TOP)


def decoded(number_ref, scale_ref, index):
    return number_ref[index].astype(F32) * scale_ref[index]


def kernel(
    scale,
    head_hbm, flow_hbm, imp_hbm, fric_hbm, junc_hbm, count_hbm, kind_hbm, up_hbm, down_hbm, open_hbm, begin_hbm,
    weights_hbm,
    end_ref, grads_ref,
    imp_ref, fric_ref, junc_ref, count_ref, kind_ref, up_ref, down_ref, open_ref, begin_ref,
    head, flow, weights, prm, halo_out, halo_in, heads, flows, h1, q1, turned, head_end,
    start_rows, end_rows, begin, a0, a1, z_val, out_val, targets, at_own, at_in, g_own, g_in,
    d_sum, sf, sfs, rf, rfs, sn, sns, rn, rns, a_sum, b_sum, sa2, sa2s, ra2, ra2s, sb2, sb2s, rb2, rb2s,
    z_sum, sz, szs, rz, rzs,
    lsem, halo_sem, old_sem, new_sem, csend, crecv, relay_sem, first_sem, early_send, second_sem, third_sem,
):
    seg, samp, zpos = lax.axis_index("seg"), lax.axis_index("samp"), lax.axis_index("dp")
    y, xlo, core = seg // 4, (seg // 2) % 2, seg % 2
    x = samp * 2 + xlo
    position = seg * 2 + samp

    def at_plane(t):
        return {"seg": t // 2, "samp": t % 2}

    def neighbour(offset):
        tx = (x + offset[1]) % 4
        return ((y + offset[0]) % 4) * 8 + (tx % 2) * 4 + ((core + offset[2]) % 2) * 2 + tx // 2

    def at_x(t):
        return {"seg": y * 4 + (t % 2) * 2 + core, "samp": t // 2}

    def at_y(t):
        return {"seg": t * 4 + xlo * 2 + core}

    def at_z(t):
        return {"dp": t}

    at_core = {"seg": y * 4 + xlo * 2 + 1 - core}

    def remote(src, dst, send, recv, device):
        return pltpu.make_async_remote_copy(
            src_ref=src, dst_ref=dst, send_sem=send, recv_sem=recv, device_id=device, device_id_type=MESH
        )

    def take(ref, sem):
        pltpu.make_async_copy(ref, ref, sem).wait()

    barrier = pltpu.get_barrier_semaphore()

    for p in (4, 3, 5, 2, 6, 1, 7):
        pl.semaphore_signal(barrier, inc=1, device_id=at_z((zpos + p) % 8), device_id_type=MESH)
    for offset in far_first():
        pl.semaphore_signal(barrier, inc=1, device_id=at_plane(neighbour(offset)), device_id_type=MESH)

    loads = [
        pltpu.make_async_copy(source, target, lsem.at[3 + number])
        for number, (source, target) in enumerate(
            (
                (head_hbm, head), (flow_hbm, flow), (imp_hbm, imp_ref), (fric_hbm, fric_ref), (junc_hbm, junc_ref),
                (count_hbm, count_ref), (kind_hbm, kind_ref), (up_hbm, up_ref), (down_hbm, down_ref),
                (open_hbm, open_ref), (begin_hbm, begin_ref), (weights_hbm, weights),
            )
        )
    ]
    for c in loads[:11]:
        c.start()

    pl.semaphore_wait(barrier, 38)

    def block(t):
        return pl.ds(pl.multiple_of(t * 64, 64), 64)

    def spread(source, target, sem, t):
        return remote(source.at[block(t)], target.at[position], sem.at[0], sem.at[1], at_plane(t))

    def send_old(offset):
        spread(head_hbm, start_rows, old_sem, neighbour(offset)).start()

    for offset in far_first()[:EARLY]:
        send_old(offset)

    row, lane = iota((16, 256), 0), iota((16, 256), 1)
    pick = jnp.where((row < 4) & (lane == jnp.where(row < 2, row, row + 252)), 1.0, 0.0).astype(BF16)
    halo_out[...] = jnp.zeros_like(halo_out)
    loads[0].wait()
    edge = dot(pick, head[...], 1, 1)
    halo_out[0, 0:2] = edge[0:2]
    halo_out[1, 0:2] = edge[2:4]
    loads[1].wait()
    edge = dot(pick, flow[...], 1, 1)
    halo_out[0, 2:4] = edge[0:2]
    halo_out[1, 2:4] = edge[2:4]

    below, above = (position + PLANE - 1) % PLANE, (position + 1) % PLANE
    halos = [
        remote(halo_out.at[0], halo_in.at[0], halo_sem.at[0], halo_sem.at[1], at_plane(below)),
        remote(halo_out.at[1], halo_in.at[1], halo_sem.at[0], halo_sem.at[1], at_plane(above)),
    ]
    for c in halos:
        c.start()

    for offset in far_first()[EARLY:]:
        send_old(offset)
    loads[11].start()
    keep_old = pltpu.make_async_copy(head.at[block(position)], start_rows.at[position], lsem.at[0])
    keep_old.start()

    for c in loads[2:11]:
        c.wait()
    prepare_params(position, imp_ref, fric_ref, junc_ref, count_ref, kind_ref, up_ref, down_ref, open_ref, prm)
    lanes = pl.ds(pl.multiple_of((position // 2) * 128, 128), 128)
    own_begin = jnp.broadcast_to(begin_ref[:, lanes].astype(F32), (64, 128))
    chosen = iota((64, 128), 1) == iota((64, 128), 0) + (position % 2) * 64
    own_begin = jnp.sum(jnp.where(chosen, own_begin, 0.0), axis=1, keepdims=True)
    begin[...] = jnp.broadcast_to(own_begin, (64, 128)).astype(jnp.int32)
    unit = eye(256)

    def turn(t, c):
        rows = pl.ds(pl.multiple_of(t * 128, 128), 128)
        heads[t, 8:264, :] = dot(unit, head[rows, :], 1, 1)
        flows[t, 8:264, :] = dot(unit, flow[rows, :], 1, 1)
        return c

    lax.fori_loop(0, 16, turn, 0)
    take(halo_in, halo_sem.at[1])

    small = eye(128)

    def one_tile(i, c):
        turn_y = (2 + 3 * (i % 4)) % 4
        tile = ((y + turn_y) % 4) * 4 + (xlo * 2 + core + 2 + i // 4 + i) % 4
        lanes = pl.ds(pl.multiple_of(tile * 128, 128), 128)
        heads[tile, 264:266, :] = halo_in[0, 0:2, lanes]
        flows[tile, 264:266, :] = halo_in[0, 2:4, lanes]
        heads[tile, 6:8, :] = halo_in[1, 0:2, lanes]
        flows[tile, 6:8, :] = halo_in[1, 2:4, lanes]
        stencil_tile(position, tile, prm, heads, flows, h1, q1, turned)
        head_end[pl.ds(pl.multiple_of(tile * 128, 128), 128), :] = dot(small, turned[...], 1, 1).astype(BF16)
        for k in range(2):
            t = 2 * tile + k

            @pl.when(t != position)
            def _():
                spread(head_end, end_rows, new_sem, t).start()

        return c

    lax.fori_loop(0, 16, one_tile, 0)
    keep_new = pltpu.make_async_copy(head_end.at[block(position)], end_rows.at[position], lsem.at[1])
    keep_new.start()
    store_end = pltpu.make_async_copy(head_end, end_ref, lsem.at[2])
    store_end.start()

    loads[11].wait()
    keep_old.wait()

    take(start_rows.at[pl.ds(0, PLANE - 1)], old_sem.at[1])
    cut_windows(start_rows, begin, a0)
    for c in range(4):
        cols = slice(c * 256, c * 256 + 256)
        z = dot(a0[...], weights[0, :, cols], 1, 0)
        z_val[:, cols] = z
        a1[:, cols] = (z * jax.nn.sigmoid(z)).astype(BF16)
    for c in range(4):
        cols = slice(c * 256, c * 256 + 256)
        out_val[:, cols] = dot(a1[...], weights[1, :, cols], 1, 0)

    def turn_a(b, c):
        cols = pl.ds(pl.multiple_of(b * 128, 128), 128)
        for layer, source in ((0, a0), (1, a1)):
            both = source[:, cols].T
            at_own[layer, 0, b] = both[0:64]
            at_own[layer, 1, b] = both[64:128]
        return c

    lax.fori_loop(0, 8, turn_a, 0)
    core_a = remote(at_own.at[:, 1 - core], at_in, csend.at[0], crecv.at[0], at_core)
    core_a.start()

    keep_new.wait()

    take(end_rows.at[pl.ds(0, PLANE - 1)], new_sem.at[1])
    cut_windows(end_rows, begin, targets)

    def to_core(layer, side):
        half = pl.ds(side * 512, 512)
        k = 1 + layer * 2 + side
        copy = remote(g_own.at[layer, :, half], g_in.at[layer, :, half], csend.at[k], crecv.at[k], at_core)
        copy.start()
        return copy

    core_g = {}
    for side in range(2):
        half = slice(side * 512, side * 512 + 512)
        g_own[1, :, half] = ((out_val[:, half] - targets[:, half].astype(F32)) * scale).astype(BF16)
        core_g[1, side] = to_core(1, side)

    def share(layer, side, target, i):
        if side == 0:
            return d_sum[layer * 8 + i * 2 + target % 2, pl.ds(pl.multiple_of((target // 2) * 32, 32), 32), 0:512]
        return d_sum[layer * 8 + target * 2 + i % 2, pl.ds(pl.multiple_of((i // 2) * 32, 32), 32), 512:1024]

    def way(layer, side, step, source, target, first, forth):
        here, at = (x, at_x) if side == 0 else (y, at_y)
        device = at((here + (1 if forth else 3)) % 4)
        part = pl.ds(first, 2)
        lane = 0 if forth else 1
        sem = relay_sem if step == 0 else first_sem
        for k in range(2):
            remote(
                source[k].at[side, lane, part],
                target[k].at[side, lane, part],
                early_send.at[k if step == 0 else 2 + k],
                sem.at[layer, side, k],
                device,
            ).start()

    def begin_exchange(layer, side):
        here = x if side == 0 else y
        base = layer * 4

        def far(i, c):
            numbers, scales = coded(share(layer, side, (here + 2) % 4, i))
            lane = i // 2
            sf[side, lane, base + i], sfs[side, lane, base + i] = numbers, scales
            return c

        lax.fori_loop(0, 4, far, 0)
        way(layer, side, 0, (sf, sfs), (rf, rfs), base, True)
        way(layer, side, 0, (sf, sfs), (rf, rfs), base + 2, False)

        def near(i, c):
            sn[side, 0, base + 2 + i], sns[side, 0, base + 2 + i] = coded(share(layer, side, (here + 1) % 4, 2 + i))
            sn[side, 1, base + i], sns[side, 1, base + i] = coded(share(layer, side, (here + 3) % 4, i))
            return c

        lax.fori_loop(0, 2, near, 0)
        way(layer, side, 1, (sn, sns), (rn, rns), base + 2, True)
        way(layer, side, 1, (sn, sns), (rn, rns), base, False)

    def pass_on(layer, side):
        here = x if side == 0 else y
        base = layer * 4
        take(rf.at[side, :, pl.ds(base, 2)], relay_sem.at[layer, side, 0])
        take(rfs.at[side, :, pl.ds(base, 2)], relay_sem.at[layer, side, 1])

        def add(i, c):
            at = base + i
            up = share(layer, side, (here + 1) % 4, i) + rf[side, 0, at].astype(F32) * rfs[side, 0, at]
            sn[side, 0, at], sns[side, 0, at] = coded(up)
            at = base + 2 + i
            down = share(layer, side, (here + 3) % 4, 2 + i) + rf[side, 1, at].astype(F32) * rfs[side, 1, at]
            sn[side, 1, at], sns[side, 1, at] = coded(down)
            return c

        lax.fori_loop(0, 2, add, 0)
        way(layer, side, 2, (sn, sns), (rn, rns), base, True)
        way(layer, side, 2, (sn, sns), (rn, rns), base + 2, False)

    def product(layer, c, left, right):
        cols = slice(c * 256, c * 256 + 256)
        return dot(left.reshape(512, 256), right[layer, :, cols], 1, 0).reshape(8, 64, 256)

    def own_product(layer):
        for c in range(4):
            d_sum[layer * 8 : layer * 8 + 8, :, c * 256 : c * 256 + 256] = product(
                layer, c, at_own[layer, core], g_own
            )

    def add_product(layer, side):
        for c in (2 * side, 2 * side + 1):
            d_sum[layer * 8 : layer * 8 + 8, :, c * 256 : c * 256 + 256] += product(layer, c, at_in[layer], g_in)

    own_product(1)
    core_a.wait_recv()
    core_g[1, 0].wait_recv()
    add_product(1, 0)
    begin_exchange(1, 0)
    core_g[1, 1].wait_recv()
    add_product(1, 1)
    begin_exchange(1, 1)
    for c in range(4):
        cols = slice(c * 256, c * 256 + 256)
        back = dot(g_own[1], weights[1, cols, :], 1, 1)
        z = z_val[:, cols]
        sigma = jax.nn.sigmoid(z)
        g_own[0, :, cols] = (back * sigma * (1.0 + z * (1.0 - sigma))).astype(BF16)
        if c % 2:
            core_g[0, c // 2] = to_core(0, c // 2)
    own_product(0)
    core_g[0, 0].wait_recv()
    add_product(0, 0)
    begin_exchange(0, 0)
    core_g[0, 1].wait_recv()
    add_product(0, 1)
    begin_exchange(0, 1)
    pass_on(1, 0)
    pass_on(1, 1)
    pass_on(0, 0)
    pass_on(0, 1)

    for layer in (1, 0):
        for side in range(2):
            take(rn.at[side, :, pl.ds(layer * 4, 4)], first_sem.at[layer, side, 0])
            take(rns.at[side, :, pl.ds(layer * 4, 4)], first_sem.at[layer, side, 1])

            def add_up(i, c, layer=layer, side=side):
                at = layer * 4 + i
                total = share(layer, side, y if side else x, i)
                for lane in range(2):
                    total = total + rn[side, lane, at].astype(F32) * rns[side, lane, at]
                if side == 0:
                    a_sum[at] = total
                    sa2[i, layer], sa2s[i, layer] = coded(total)
                else:
                    b_sum[at] = total
                    sb2[i, layer], sb2s[i, layer] = coded(total)
                return c

            lax.fori_loop(0, 4, add_up, 0)
            for p in (2, 1, 3):
                tx, ty = (x + p) % 4, (y + p) % 4
                parts = (
                    ((sa2, ra2, ty, at_y(ty)), (sa2s, ra2s, ty, at_y(ty)))
                    if side == 0
                    else ((sb2, rb2, tx, at_x(tx)), (sb2s, rb2s, tx, at_x(tx)))
                )
                for k, (source, target, t, device) in enumerate(parts):
                    k = 2 * side + k
                    remote(
                        source.at[t, layer], target.at[p - 1, layer], second_sem.at[0, k], second_sem.at[1, k], device
                    ).start()
    for k, ref in enumerate((ra2, ra2s, rb2, rb2s)):
        take(ref, second_sem.at[1, k])

    for layer in range(2):
        left = a_sum[layer * 4 + y]
        right = b_sum[layer * 4 + x]
        for p in range(3):
            left = left + ra2[p, layer].astype(F32) * ra2s[p, layer]
            right = right + rb2[p, layer].astype(F32) * rb2s[p, layer]
        for t in range(8):
            z_sum[t, 4 * layer : 4 * layer + 4] = left[4 * t : 4 * t + 4]
            z_sum[t, 8 + 4 * layer : 12 + 4 * layer] = right[4 * t : 4 * t + 4]
    for t in range(8):
        sz[t], szs[t] = coded(z_sum[t])
    for p in (4, 3, 5, 2, 6, 1, 7):
        t = (zpos + p) % 8
        remote(sz.at[t], rz.at[p - 1], third_sem.at[0, 0], third_sem.at[1, 0], at_z(t)).start()
        remote(szs.at[t], rzs.at[p - 1], third_sem.at[0, 1], third_sem.at[1, 1], at_z(t)).start()
    take(rz, third_sem.at[1, 0])
    take(rzs, third_sem.at[1, 1])
    total = z_sum[zpos]
    for p in range(7):
        total = total + rz[p].astype(F32) * rzs[p]
    for layer in range(2):
        grads_ref[layer, :, 0:512] = total[4 * layer : 4 * layer + 4]
        grads_ref[layer, :, 512:1024] = total[8 + 4 * layer : 12 + 4 * layer]
    take(halo_out, halo_sem.at[0])
    take(start_rows.at[pl.ds(0, PLANE - 1)], old_sem.at[0])
    take(end_rows.at[pl.ds(0, PLANE - 1)], new_sem.at[0])
    core_a.wait_send()
    for c in core_g.values():
        c.wait_send()
    for k, ref in enumerate((sf.at[0], sfs.at[0], sn, sns)):
        take(ref, early_send.at[k])
    for k, ref in enumerate((ra2, ra2s, rb2, rb2s)):
        take(ref, second_sem.at[0, k])
    take(rz, third_sem.at[0, 0])
    take(rzs, third_sem.at[0, 1])
    store_end.wait()


def whole(scale, *operands):
    hbm = pl.BlockSpec(memory_space=pl.ANY)
    vmem = pl.BlockSpec(memory_space=pltpu.VMEM)
    dma = pltpu.SemaphoreType.DMA
    return pl.pallas_call(
        functools.partial(kernel, scale),
        out_shape=[
            jax.ShapeDtypeStruct((2048, 256), BF16),
            jax.ShapeDtypeStruct((2, 4, 1024), F32),
        ],
        in_specs=[hbm] * 12,
        out_specs=[hbm, vmem],
        scratch_shapes=[
            pltpu.VMEM((8, 2048), F32),
            pltpu.VMEM((8, 2048), F32),
            pltpu.VMEM((8, 2048), jnp.int32),
            pltpu.VMEM((1, 2048), jnp.int32),
            pltpu.VMEM((1, 2048), jnp.int32),
            pltpu.VMEM((1, 2048), F32),
            pltpu.VMEM((1, 2048), F32),
            pltpu.VMEM((1, 2048), F32),
            pltpu.VMEM((1, 2048), jnp.int32),
            pltpu.VMEM((2048, 256), BF16),
            pltpu.VMEM((2048, 256), BF16),
            pltpu.VMEM((2, 1024, 1024), BF16),
            pltpu.VMEM((16, 2048), F32),
            pltpu.VMEM((2, 8, 2048), F32),
            pltpu.VMEM((2, 8, 2048), F32),
            pltpu.VMEM((16, 272, 128), F32),
            pltpu.VMEM((16, 272, 128), F32),
            pltpu.VMEM((264, 128), F32),
            pltpu.VMEM((264, 128), F32),
            pltpu.VMEM((256, 128), BF16),
            pltpu.VMEM((2048, 256), BF16),
            pltpu.VMEM((32, 64, 256), BF16),
            pltpu.VMEM((32, 64, 256), BF16),
            pltpu.VMEM((64, 128), jnp.int32),
            pltpu.VMEM((256, 1024), BF16),
            pltpu.VMEM((256, 1024), BF16),
            pltpu.VMEM((256, 1024), F32),
            pltpu.VMEM((256, 1024), F32),
            pltpu.VMEM((256, 1024), BF16),
            pltpu.VMEM((2, 2, 8, 64, 256), BF16),
            pltpu.VMEM((2, 8, 64, 256), BF16),
            pltpu.VMEM((2, 256, 1024), BF16),
            pltpu.VMEM((2, 256, 1024), BF16),
            pltpu.VMEM((16, 64, 1024), F32),
            pltpu.VMEM((2, 2, 8, 32, 512), I16),
            pltpu.VMEM((2, 2, 8, 1, 512), F32),
            pltpu.VMEM((2, 2, 8, 32, 512), I16),
            pltpu.VMEM((2, 2, 8, 1, 512), F32),
            pltpu.VMEM((2, 2, 8, 32, 512), I16),
            pltpu.VMEM((2, 2, 8, 1, 512), F32),
            pltpu.VMEM((2, 2, 8, 32, 512), I16),
            pltpu.VMEM((2, 2, 8, 1, 512), F32),
            pltpu.VMEM((8, 32, 512), F32),
            pltpu.VMEM((8, 32, 512), F32),
            pltpu.VMEM((4, 2, 32, 512), I16),
            pltpu.VMEM((4, 2, 1, 512), F32),
            pltpu.VMEM((3, 2, 32, 512), I16),
            pltpu.VMEM((3, 2, 1, 512), F32),
            pltpu.VMEM((4, 2, 32, 512), I16),
            pltpu.VMEM((4, 2, 1, 512), F32),
            pltpu.VMEM((3, 2, 32, 512), I16),
            pltpu.VMEM((3, 2, 1, 512), F32),
            pltpu.VMEM((8, 16, 512), F32),
            pltpu.VMEM((8, 16, 512), I16),
            pltpu.VMEM((8, 1, 512), F32),
            pltpu.VMEM((7, 16, 512), I16),
            pltpu.VMEM((7, 1, 512), F32),
            dma((15,)),
            dma((2,)),
            dma((2,)),
            dma((2,)),
            dma((5,)),
            dma((5,)),
            dma((2, 2, 2)),
            dma((2, 2, 2)),
            dma((4,)),
            dma((2, 4)),
            dma((2, 2)),
        ],
        compiler_params=pltpu.CompilerParams(
            collective_id=1, has_side_effects=True, vmem_limit_bytes=58 << 20
        ),
    )(*operands)


def finish_kernel(end_ref, grads_ref, end_out, grads_out, held, totals, load_sem, store_sem):
    parts = [pl.ds(i * 512, 512) for i in range(4)]
    loads = [pltpu.make_async_copy(end_ref.at[r], held.at[r], load_sem.at[i]) for i, r in enumerate(parts)]
    stores = [pltpu.make_async_copy(held.at[r], end_out.at[r], store_sem.at[i]) for i, r in enumerate(parts)]
    loads.append(pltpu.make_async_copy(grads_ref, totals, load_sem.at[4]))
    stores.append(pltpu.make_async_copy(totals, grads_out, store_sem.at[4]))
    for c in loads:
        c.start()
    for load, store in zip(loads, stores):
        load.wait()
        store.start()
    for c in stores:
        c.wait()


def finish(end, grads):
    hbm = pl.BlockSpec(memory_space=pl.ANY)
    return pl.pallas_call(
        finish_kernel,
        out_shape=[jax.ShapeDtypeStruct(end.shape, end.dtype), jax.ShapeDtypeStruct(grads.shape, grads.dtype)],
        in_specs=[hbm, hbm],
        out_specs=[hbm, hbm],
        scratch_shapes=[
            pltpu.VMEM(end.shape, end.dtype),
            pltpu.VMEM(grads.shape, grads.dtype),
            pltpu.SemaphoreType.DMA((5,)),
            pltpu.SemaphoreType.DMA((5,)),
        ],
        compiler_params=pltpu.CompilerParams(vmem_limit_bytes=58 << 20),
    )(end, grads)


def body(
    head_start,
    flow_start,
    impedance,
    friction,
    seg_count,
    junction_code,
    boundary_code,
    head_up,
    head_down,
    opening,
    window_start,
    layer_weights,
):
    row_total = window_start.shape[0] * lax.axis_size("dp") * 4
    return tuple(
        finish(
            *whole(
            8.0 / row_total,
            head_start,
            flow_start,
            impedance.T,
            friction.T,
            junction_code.T,
            seg_count[None, :],
            boundary_code[None, :],
            head_up[None, :],
            head_down[None, :],
            opening[None, :],
            window_start[None, :],
            layer_weights,
        ))
    )


def solution(mesh):
    placed = (
        P("dp", ("seg", "samp")),
        P("dp", ("seg", "samp")),
        P("dp", None),
        P("dp", None),
        P("dp"),
        P("dp", None),
        P("dp"),
        P("dp"),
        P("dp"),
        P("dp"),
        P("dp"),
        P(),
    )
    return jax.shard_map(
        body,
        mesh=mesh,
        in_specs=placed,
        out_specs=(P("dp", ("seg", "samp")), P(None, ("seg", "samp", "dp"), None)),
        check_vma=False,
    )
```

```python
import functools
import jax
import jax.numpy as jnp
from jax import lax
from jax.experimental import pallas as pl
from jax.experimental.pallas import tpu as pltpu
from jax.sharding import PartitionSpec as P

MESH = pl.DeviceIdType.MESH
PLANE = 32
CELLS = 8192
BF16 = jnp.bfloat16
F32 = jnp.float32
I16 = jnp.int16
TOP = 32767.0
EARLY = 10


def dot(lhs, rhs, lhs_dim, rhs_dim):
    return lax.dot_general(
        lhs, rhs, (((lhs_dim,), (rhs_dim,)), ((), ())), preferred_element_type=F32
    )


def iota(shape, dim):
    return lax.broadcasted_iota(jnp.int32, shape, dim)


def far_first():
    offsets = [(dy, dx, dc) for dy in range(4) for dx in range(4) for dc in range(2)][1:]

    def key(offset):
        dy, dx, dc = offset
        return (min(dy, 4 - dy) + min(dx, 4 - dx), dc, (dx * 7 + dy * 3) % 5)

    return sorted(offsets, key=key, reverse=True)


def eye(size):
    return jnp.where(iota((size, size), 0) == iota((size, size), 1), 1.0, 0.0).astype(BF16)


W_LO, W_HI, L_LO, L_HI, H_LO, H_HI, FIRST, COUNT, END_A, END_L, END_Q, UPPER = range(12)


def prepare_params(position, imp_ref, fric_ref, junc_ref, count_ref, kind_ref, up_ref, down_ref, open_ref, prm):
    wide = imp_ref.shape
    imp = imp_ref[...]
    loss = fric_ref[...] * (1.0 + junc_ref[...].astype(F32))
    count = count_ref[...]
    before = position * 256 - 1
    section = lax.shift_right_logical(jnp.maximum(before, 0) * count, 13)
    row = iota(wide, 0)

    def pick(values, number):
        return jnp.sum(jnp.where(row == number, values, 0.0), axis=0, keepdims=True)

    w_lo, w_hi = pick(imp, section), pick(imp, section + 1)
    w_end = pick(imp, count - 1)
    prm[W_LO : W_LO + 1] = w_lo
    prm[W_HI : W_HI + 1] = w_hi
    prm[L_LO : L_LO + 1] = pick(loss, section)
    prm[L_HI : L_HI + 1] = pick(loss, section + 1)
    prm[H_LO : H_LO + 1] = 0.5 / w_lo
    prm[H_HI : H_HI + 1] = 0.5 / jnp.where(w_hi == 0.0, 1.0, w_hi)
    prm[FIRST : FIRST + 1] = (before * count - (section + 1) * CELLS).astype(F32)
    prm[COUNT : COUNT + 1] = count.astype(F32)
    kind, valve = kind_ref[...], open_ref[...]
    factor = 1.0 / (1.0 + w_end * valve)
    prm[END_A : END_A + 1] = jnp.where(kind == 0, 0.0, jnp.where(kind == 1, 1.0, factor))
    prm[END_L : END_L + 1] = jnp.where(kind == 0, down_ref[...], 0.0)
    prm[END_Q : END_Q + 1] = jnp.where(kind == 0, 1.0 / w_end, jnp.where(kind == 1, 0.0, valve * factor))
    prm[UPPER : UPPER + 1] = up_ref[...]


def stencil_tile(position, tile, prm, heads, flows, h1, q1, turned):
    lanes = pl.ds(pl.multiple_of(tile * 128, 128), 128)

    def param(number, rows=8):
        return jnp.broadcast_to(prm[number : number + 1, lanes], (rows, 128))

    count = param(COUNT)
    start = param(FIRST) + iota((8, 128), 0).astype(F32) * count
    lows = [param(W_LO), param(L_LO), param(H_LO)]
    highs = [param(W_HI), param(L_HI), param(H_HI)]

    def fields(value, number):
        high = value >= 0.0
        return [jnp.where(high, highs[k], lows[k]) for k in range(number)]

    def ends(lh, lq, rh, rq, wave, loss):
        forward = lh + lq * (wave - loss * jnp.abs(lq))
        backward = rh - rq * (wave - loss * jnp.abs(rq))
        return forward, backward

    def first(g, value):
        wave, loss, half = fields(value, 3)
        left, right = pl.ds(8 * g + 6, 8), pl.ds(8 * g + 8, 8)
        forward, backward = ends(
            heads[tile, left, :], flows[tile, left, :], heads[tile, right, :], flows[tile, right, :], wave, loss
        )
        return forward, backward, half

    value = start
    for g in range(33):
        forward, backward, half = first(g, value)
        h1[8 * g : 8 * g + 8] = 0.5 * (forward + backward)
        q1[8 * g : 8 * g + 8] = (forward - backward) * half
        value = value + 8.0 * count

    @pl.when(position == 0)
    def _():
        _, backward, half = first(0, start)
        upper = param(UPPER)
        at = iota((8, 128), 0) == 1
        h1[0:8] = jnp.where(at, upper, h1[0:8])
        q1[0:8] = jnp.where(at, (upper - backward) * (2.0 * half), q1[0:8])

    @pl.when(position == PLANE - 1)
    def _():
        forward, _, _ = first(32, start + 256.0 * count)
        at = iota((8, 128), 0) == 0
        h1[256:264] = jnp.where(at, param(END_A) * forward + param(END_L), h1[256:264])
        q1[256:264] = jnp.where(at, (forward - param(END_L)) * param(END_Q), q1[256:264])

    def second(g, value):
        wave, loss = fields(value, 2)
        left, right = pl.ds(8 * g, 8), pl.ds(8 * g + 2, 8)
        return ends(h1[left, :], q1[left, :], h1[right, :], q1[right, :], wave, loss)

    value = start + count
    for g in range(16):
        pieces = []
        for _ in range(2):
            forward, backward = second(2 * g + len(pieces), value)
            pieces.append(0.5 * (forward + backward))
            value = value + 8.0 * count
        turned[16 * g : 16 * g + 16] = jnp.concatenate(pieces, axis=0).astype(BF16)

    @pl.when(position == 0)
    def _():
        at = iota((16, 128), 0) == 0
        turned[0:16] = jnp.where(at, param(UPPER, 16), turned[0:16].astype(F32)).astype(BF16)

    @pl.when(position == PLANE - 1)
    def _():
        forward, _ = second(31, start + 249.0 * count)
        last = param(END_A) * forward + param(END_L)
        last = jnp.concatenate([last, last], axis=0)
        at = iota((16, 128), 0) == 15
        turned[240:256] = jnp.where(at, last, turned[240:256].astype(F32)).astype(BF16)


def cut_windows(rows_ref, begin_ref, out_ref):
    def group(number, carry):
        here = pl.ds(pl.multiple_of(number * 16, 16), 16)
        begin = begin_ref[here, :]
        block = lax.shift_right_logical(begin, 7).astype(I16)
        rest = begin & 127
        lane = iota((16, 128), 1)
        values = []
        for source in range(PLANE):
            pair = rows_ref[source, here, :]
            values += [pair[:, :128], pair[:, 128:]]
        for bit, count in ((32, 64), (16, 48), (8, 40), (4, 36), (2, 34), (1, 33)):
            on = (block & jnp.int16(bit)) != 0
            values = [
                jnp.where(on, values[j + bit], values[j]) if j + bit < len(values) else values[j]
                for j in range(count)
            ]
        index = (lane + rest) & 127
        keep = lane + rest < 128
        moved = [jnp.take_along_axis(v.astype(F32), index, axis=1) for v in values]
        for j in range(32):
            piece = jnp.where(keep, moved[j], moved[j + 1]).astype(BF16)
            at = pl.ds(pl.multiple_of((j // 8) * 64 + number * 16, 16), 16)
            out_ref[at, (j % 8) * 128 : (j % 8) * 128 + 128] = piece
        return carry

    lax.fori_loop(0, 4, group, 0)


def coded(block):
    top = jnp.maximum(jnp.max(jnp.abs(block), axis=0, keepdims=True), 1e-30)
    return jnp.round(block * (TOP / top)).astype(I16), top * (1.0 / TOP)


def decoded(number_ref, scale_ref, index):
    return number_ref[index].astype(F32) * scale_ref[index]


def kernel(
    scale,
    head_hbm, flow_hbm, imp_hbm, fric_hbm, junc_hbm, count_hbm, kind_hbm, up_hbm, down_hbm, open_hbm, begin_hbm,
    weights_hbm,
    end_ref, grads_ref,
    imp_ref, fric_ref, junc_ref, count_ref, kind_ref, up_ref, down_ref, open_ref, begin_ref,
    head, flow, weights, prm, halo_out, halo_in, heads, flows, h1, q1, turned, head_end,
    start_rows, end_rows, begin, a0, a1, z_val, out_val, targets, at_own, at_in, g_own, g_in,
    d_sum, sf, sfs, rf, rfs, sn, sns, rn, rns, a_sum, b_sum, sa2, sa2s, ra2, ra2s, sb2, sb2s, rb2, rb2s,
    z_sum, sz, szs, rz, rzs,
    lsem, halo_sem, old_sem, new_sem, csend, crecv, relay_sem, first_sem, early_send, second_sem, third_sem,
):
    seg, samp, zpos = lax.axis_index("seg"), lax.axis_index("samp"), lax.axis_index("dp")
    y, xlo, core = seg // 4, (seg // 2) % 2, seg % 2
    x = samp * 2 + xlo
    position = seg * 2 + samp

    def at_plane(t):
        return {"seg": t // 2, "samp": t % 2}

    def neighbour(offset):
        tx = (x + offset[1]) % 4
        return ((y + offset[0]) % 4) * 8 + (tx % 2) * 4 + ((core + offset[2]) % 2) * 2 + tx // 2

    def at_x(t):
        return {"seg": y * 4 + (t % 2) * 2 + core, "samp": t // 2}

    def at_y(t):
        return {"seg": t * 4 + xlo * 2 + core}

    def at_z(t):
        return {"dp": t}

    at_core = {"seg": y * 4 + xlo * 2 + 1 - core}

    def remote(src, dst, send, recv, device):
        return pltpu.make_async_remote_copy(
            src_ref=src, dst_ref=dst, send_sem=send, recv_sem=recv, device_id=device, device_id_type=MESH
        )

    def take(ref, sem):
        pltpu.make_async_copy(ref, ref, sem).wait()

    barrier = pltpu.get_barrier_semaphore()

    for p in (4, 3, 5, 2, 6, 1, 7):
        pl.semaphore_signal(barrier, inc=1, device_id=at_z((zpos + p) % 8), device_id_type=MESH)
    for offset in far_first():
        pl.semaphore_signal(barrier, inc=1, device_id=at_plane(neighbour(offset)), device_id_type=MESH)

    loads = [
        pltpu.make_async_copy(source, target, lsem.at[3 + number])
        for number, (source, target) in enumerate(
            (
                (head_hbm, head), (flow_hbm, flow), (imp_hbm, imp_ref), (fric_hbm, fric_ref), (junc_hbm, junc_ref),
                (count_hbm, count_ref), (kind_hbm, kind_ref), (up_hbm, up_ref), (down_hbm, down_ref),
                (open_hbm, open_ref), (begin_hbm, begin_ref), (weights_hbm, weights),
            )
        )
    ]
    for c in loads[:11]:
        c.start()

    pl.semaphore_wait(barrier, 38)

    def block(t):
        return pl.ds(pl.multiple_of(t * 64, 64), 64)

    def spread(source, target, sem, t):
        return remote(source.at[block(t)], target.at[position], sem.at[0], sem.at[1], at_plane(t))

    def send_old(offset):
        spread(head_hbm, start_rows, old_sem, neighbour(offset)).start()

    for offset in far_first()[:EARLY]:
        send_old(offset)

    row, lane = iota((16, 256), 0), iota((16, 256), 1)
    pick = jnp.where((row < 4) & (lane == jnp.where(row < 2, row, row + 252)), 1.0, 0.0).astype(BF16)
    halo_out[...] = jnp.zeros_like(halo_out)
    loads[0].wait()
    edge = dot(pick, head[...], 1, 1)
    halo_out[0, 0:2] = edge[0:2]
    halo_out[1, 0:2] = edge[2:4]
    loads[1].wait()
    edge = dot(pick, flow[...], 1, 1)
    halo_out[0, 2:4] = edge[0:2]
    halo_out[1, 2:4] = edge[2:4]

    below, above = (position + PLANE - 1) % PLANE, (position + 1) % PLANE
    halos = [
        remote(halo_out.at[0], halo_in.at[0], halo_sem.at[0], halo_sem.at[1], at_plane(below)),
        remote(halo_out.at[1], halo_in.at[1], halo_sem.at[0], halo_sem.at[1], at_plane(above)),
    ]
    for c in halos:
        c.start()

    for offset in far_first()[EARLY:]:
        send_old(offset)
    loads[11].start()
    keep_old = pltpu.make_async_copy(head.at[block(position)], start_rows.at[position], lsem.at[0])
    keep_old.start()

    for c in loads[2:11]:
        c.wait()
    prepare_params(position, imp_ref, fric_ref, junc_ref, count_ref, kind_ref, up_ref, down_ref, open_ref, prm)
    lanes = pl.ds(pl.multiple_of((position // 2) * 128, 128), 128)
    own_begin = jnp.broadcast_to(begin_ref[:, lanes].astype(F32), (64, 128))
    chosen = iota((64, 128), 1) == iota((64, 128), 0) + (position % 2) * 64
    own_begin = jnp.sum(jnp.where(chosen, own_begin, 0.0), axis=1, keepdims=True)
    begin[...] = jnp.broadcast_to(own_begin, (64, 128)).astype(jnp.int32)
    unit = eye(256)

    def turn(t, c):
        rows = pl.ds(pl.multiple_of(t * 128, 128), 128)
        heads[t, 8:264, :] = dot(unit, head[rows, :], 1, 1)
        flows[t, 8:264, :] = dot(unit, flow[rows, :], 1, 1)
        return c

    lax.fori_loop(0, 16, turn, 0)
    take(halo_in, halo_sem.at[1])

    small = eye(128)

    def one_tile(i, c):
        turn_y = (2 + 3 * (i % 4)) % 4
        tile = ((y + turn_y) % 4) * 4 + (xlo * 2 + core + 2 + i // 4 + i) % 4
        lanes = pl.ds(pl.multiple_of(tile * 128, 128), 128)
        heads[tile, 264:266, :] = halo_in[0, 0:2, lanes]
        flows[tile, 264:266, :] = halo_in[0, 2:4, lanes]
        heads[tile, 6:8, :] = halo_in[1, 0:2, lanes]
        flows[tile, 6:8, :] = halo_in[1, 2:4, lanes]
        stencil_tile(position, tile, prm, heads, flows, h1, q1, turned)
        head_end[pl.ds(pl.multiple_of(tile * 128, 128), 128), :] = dot(small, turned[...], 1, 1).astype(BF16)
        for k in range(2):
            t = 2 * tile + k

            @pl.when(t != position)
            def _():
                spread(head_end, end_rows, new_sem, t).start()

        return c

    lax.fori_loop(0, 16, one_tile, 0)
    keep_new = pltpu.make_async_copy(head_end.at[block(position)], end_rows.at[position], lsem.at[1])
    keep_new.start()
    store_end = pltpu.make_async_copy(head_end, end_ref, lsem.at[2])
    store_end.start()

    loads[11].wait()
    keep_old.wait()

    take(start_rows.at[pl.ds(0, PLANE - 1)], old_sem.at[1])
    cut_windows(start_rows, begin, a0)
    for c in range(4):
        cols = slice(c * 256, c * 256 + 256)
        z = dot(a0[...], weights[0, :, cols], 1, 0)
        z_val[:, cols] = z
        a1[:, cols] = (z * jax.nn.sigmoid(z)).astype(BF16)
    for c in range(4):
        cols = slice(c * 256, c * 256 + 256)
        out_val[:, cols] = dot(a1[...], weights[1, :, cols], 1, 0)

    def turn_a(b, c):
        cols = pl.ds(pl.multiple_of(b * 128, 128), 128)
        for layer, source in ((0, a0), (1, a1)):
            both = source[:, cols].T
            at_own[layer, 0, b] = both[0:64]
            at_own[layer, 1, b] = both[64:128]
        return c

    lax.fori_loop(0, 8, turn_a, 0)
    core_a = remote(at_own.at[:, 1 - core], at_in, csend.at[0], crecv.at[0], at_core)
    core_a.start()

    keep_new.wait()

    take(end_rows.at[pl.ds(0, PLANE - 1)], new_sem.at[1])
    cut_windows(end_rows, begin, targets)

    def to_core(layer, side):
        half = pl.ds(side * 512, 512)
        k = 1 + layer * 2 + side
        copy = remote(g_own.at[layer, :, half], g_in.at[layer, :, half], csend.at[k], crecv.at[k], at_core)
        copy.start()
        return copy

    core_g = {}
    for side in range(2):
        half = slice(side * 512, side * 512 + 512)
        g_own[1, :, half] = ((out_val[:, half] - targets[:, half].astype(F32)) * scale).astype(BF16)
        core_g[1, side] = to_core(1, side)

    def share(layer, side, target, i):
        if side == 0:
            return d_sum[layer * 8 + i * 2 + target % 2, pl.ds(pl.multiple_of((target // 2) * 32, 32), 32), 0:512]
        return d_sum[layer * 8 + target * 2 + i % 2, pl.ds(pl.multiple_of((i // 2) * 32, 32), 32), 512:1024]

    def way(layer, side, step, source, target, first, forth):
        here, at = (x, at_x) if side == 0 else (y, at_y)
        device = at((here + (1 if forth else 3)) % 4)
        part = pl.ds(first, 2)
        lane = 0 if forth else 1
        sem = relay_sem if step == 0 else first_sem
        for k in range(2):
            remote(
                source[k].at[side, lane, part],
                target[k].at[side, lane, part],
                early_send.at[k if step == 0 else 2 + k],
                sem.at[layer, side, k],
                device,
            ).start()

    def begin_exchange(layer, side):
        here = x if side == 0 else y
        base = layer * 4

        def far(i, c):
            numbers, scales = coded(share(layer, side, (here + 2) % 4, i))
            lane = i // 2
            sf[side, lane, base + i], sfs[side, lane, base + i] = numbers, scales
            return c

        lax.fori_loop(0, 4, far, 0)
        way(layer, side, 0, (sf, sfs), (rf, rfs), base, True)
        way(layer, side, 0, (sf, sfs), (rf, rfs), base + 2, False)

    def direct(layer, side):
        here = x if side == 0 else y
        base = layer * 4

        def near(i, c):
            sn[side, 0, base + 2 + i], sns[side, 0, base + 2 + i] = coded(share(layer, side, (here + 1) % 4, 2 + i))
            sn[side, 1, base + i], sns[side, 1, base + i] = coded(share(layer, side, (here + 3) % 4, i))
            return c

        lax.fori_loop(0, 2, near, 0)
        way(layer, side, 1, (sn, sns), (rn, rns), base + 2, True)
        way(layer, side, 1, (sn, sns), (rn, rns), base, False)

    def pass_on(layer, side):
        here = x if side == 0 else y
        base = layer * 4
        take(rf.at[side, :, pl.ds(base, 2)], relay_sem.at[layer, side, 0])
        take(rfs.at[side, :, pl.ds(base, 2)], relay_sem.at[layer, side, 1])

        def add(i, c):
            at = base + i
            up = share(layer, side, (here + 1) % 4, i) + rf[side, 0, at].astype(F32) * rfs[side, 0, at]
            sn[side, 0, at], sns[side, 0, at] = coded(up)
            at = base + 2 + i
            down = share(layer, side, (here + 3) % 4, 2 + i) + rf[side, 1, at].astype(F32) * rfs[side, 1, at]
            sn[side, 1, at], sns[side, 1, at] = coded(down)
            return c

        lax.fori_loop(0, 2, add, 0)
        way(layer, side, 2, (sn, sns), (rn, rns), base, True)
        way(layer, side, 2, (sn, sns), (rn, rns), base + 2, False)

    def product(layer, c, left, right):
        cols = slice(c * 256, c * 256 + 256)
        return dot(left.reshape(512, 256), right[layer, :, cols], 1, 0).reshape(8, 64, 256)

    def own_product(layer):
        for c in range(4):
            d_sum[layer * 8 : layer * 8 + 8, :, c * 256 : c * 256 + 256] = product(
                layer, c, at_own[layer, core], g_own
            )

    def add_product(layer, side):
        for c in (2 * side, 2 * side + 1):
            d_sum[layer * 8 : layer * 8 + 8, :, c * 256 : c * 256 + 256] += product(layer, c, at_in[layer], g_in)

    own_product(1)
    core_a.wait_recv()
    core_g[1, 0].wait_recv()
    add_product(1, 0)
    begin_exchange(1, 0)
    core_g[1, 1].wait_recv()
    add_product(1, 1)
    begin_exchange(1, 1)
    direct(1, 0)
    direct(1, 1)
    for c in range(4):
        cols = slice(c * 256, c * 256 + 256)
        back = dot(g_own[1], weights[1, cols, :], 1, 1)
        z = z_val[:, cols]
        sigma = jax.nn.sigmoid(z)
        g_own[0, :, cols] = (back * sigma * (1.0 + z * (1.0 - sigma))).astype(BF16)
        if c % 2:
            core_g[0, c // 2] = to_core(0, c // 2)
    own_product(0)
    core_g[0, 0].wait_recv()
    add_product(0, 0)
    begin_exchange(0, 0)
    core_g[0, 1].wait_recv()
    add_product(0, 1)
    begin_exchange(0, 1)
    direct(0, 0)
    direct(0, 1)
    pass_on(1, 0)
    pass_on(1, 1)
    pass_on(0, 0)
    pass_on(0, 1)

    for layer in (1, 0):
        for side in range(2):
            take(rn.at[side, :, pl.ds(layer * 4, 4)], first_sem.at[layer, side, 0])
            take(rns.at[side, :, pl.ds(layer * 4, 4)], first_sem.at[layer, side, 1])

            def add_up(i, c, layer=layer, side=side):
                at = layer * 4 + i
                total = share(layer, side, y if side else x, i)
                for lane in range(2):
                    total = total + rn[side, lane, at].astype(F32) * rns[side, lane, at]
                if side == 0:
                    a_sum[at] = total
                    sa2[i, layer], sa2s[i, layer] = coded(total)
                else:
                    b_sum[at] = total
                    sb2[i, layer], sb2s[i, layer] = coded(total)
                return c

            lax.fori_loop(0, 4, add_up, 0)
            for p in (2, 1, 3):
                tx, ty = (x + p) % 4, (y + p) % 4
                parts = (
                    ((sa2, ra2, ty, at_y(ty)), (sa2s, ra2s, ty, at_y(ty)))
                    if side == 0
                    else ((sb2, rb2, tx, at_x(tx)), (sb2s, rb2s, tx, at_x(tx)))
                )
                for k, (source, target, t, device) in enumerate(parts):
                    k = 2 * side + k
                    remote(
                        source.at[t, layer], target.at[p - 1, layer], second_sem.at[0, k], second_sem.at[1, k], device
                    ).start()
    for k, ref in enumerate((ra2, ra2s, rb2, rb2s)):
        take(ref, second_sem.at[1, k])

    for layer in range(2):
        left = a_sum[layer * 4 + y]
        right = b_sum[layer * 4 + x]
        for p in range(3):
            left = left + ra2[p, layer].astype(F32) * ra2s[p, layer]
            right = right + rb2[p, layer].astype(F32) * rb2s[p, layer]
        for t in range(8):
            z_sum[t, 4 * layer : 4 * layer + 4] = left[4 * t : 4 * t + 4]
            z_sum[t, 8 + 4 * layer : 12 + 4 * layer] = right[4 * t : 4 * t + 4]
    for t in range(8):
        sz[t], szs[t] = coded(z_sum[t])
    for p in (4, 3, 5, 2, 6, 1, 7):
        t = (zpos + p) % 8
        remote(sz.at[t], rz.at[p - 1], third_sem.at[0, 0], third_sem.at[1, 0], at_z(t)).start()
        remote(szs.at[t], rzs.at[p - 1], third_sem.at[0, 1], third_sem.at[1, 1], at_z(t)).start()
    take(rz, third_sem.at[1, 0])
    take(rzs, third_sem.at[1, 1])
    total = z_sum[zpos]
    for p in range(7):
        total = total + rz[p].astype(F32) * rzs[p]
    for layer in range(2):
        grads_ref[layer, :, 0:512] = total[4 * layer : 4 * layer + 4]
        grads_ref[layer, :, 512:1024] = total[8 + 4 * layer : 12 + 4 * layer]
    take(halo_out, halo_sem.at[0])
    take(start_rows.at[pl.ds(0, PLANE - 1)], old_sem.at[0])
    take(end_rows.at[pl.ds(0, PLANE - 1)], new_sem.at[0])
    core_a.wait_send()
    for c in core_g.values():
        c.wait_send()
    for k, ref in enumerate((sf.at[0], sfs.at[0], sn, sns)):
        take(ref, early_send.at[k])
    for k, ref in enumerate((ra2, ra2s, rb2, rb2s)):
        take(ref, second_sem.at[0, k])
    take(rz, third_sem.at[0, 0])
    take(rzs, third_sem.at[0, 1])
    store_end.wait()


def whole(scale, *operands):
    hbm = pl.BlockSpec(memory_space=pl.ANY)
    vmem = pl.BlockSpec(memory_space=pltpu.VMEM)
    dma = pltpu.SemaphoreType.DMA
    return pl.pallas_call(
        functools.partial(kernel, scale),
        out_shape=[
            jax.ShapeDtypeStruct((2048, 256), BF16),
            jax.ShapeDtypeStruct((2, 4, 1024), F32),
        ],
        in_specs=[hbm] * 12,
        out_specs=[hbm, vmem],
        scratch_shapes=[
            pltpu.VMEM((8, 2048), F32),
            pltpu.VMEM((8, 2048), F32),
            pltpu.VMEM((8, 2048), jnp.int32),
            pltpu.VMEM((1, 2048), jnp.int32),
            pltpu.VMEM((1, 2048), jnp.int32),
            pltpu.VMEM((1, 2048), F32),
            pltpu.VMEM((1, 2048), F32),
            pltpu.VMEM((1, 2048), F32),
            pltpu.VMEM((1, 2048), jnp.int32),
            pltpu.VMEM((2048, 256), BF16),
            pltpu.VMEM((2048, 256), BF16),
            pltpu.VMEM((2, 1024, 1024), BF16),
            pltpu.VMEM((16, 2048), F32),
            pltpu.VMEM((2, 8, 2048), F32),
            pltpu.VMEM((2, 8, 2048), F32),
            pltpu.VMEM((16, 272, 128), F32),
            pltpu.VMEM((16, 272, 128), F32),
            pltpu.VMEM((264, 128), F32),
            pltpu.VMEM((264, 128), F32),
            pltpu.VMEM((256, 128), BF16),
            pltpu.VMEM((2048, 256), BF16),
            pltpu.VMEM((32, 64, 256), BF16),
            pltpu.VMEM((32, 64, 256), BF16),
            pltpu.VMEM((64, 128), jnp.int32),
            pltpu.VMEM((256, 1024), BF16),
            pltpu.VMEM((256, 1024), BF16),
            pltpu.VMEM((256, 1024), F32),
            pltpu.VMEM((256, 1024), F32),
            pltpu.VMEM((256, 1024), BF16),
            pltpu.VMEM((2, 2, 8, 64, 256), BF16),
            pltpu.VMEM((2, 8, 64, 256), BF16),
            pltpu.VMEM((2, 256, 1024), BF16),
            pltpu.VMEM((2, 256, 1024), BF16),
            pltpu.VMEM((16, 64, 1024), F32),
            pltpu.VMEM((2, 2, 8, 32, 512), I16),
            pltpu.VMEM((2, 2, 8, 1, 512), F32),
            pltpu.VMEM((2, 2, 8, 32, 512), I16),
            pltpu.VMEM((2, 2, 8, 1, 512), F32),
            pltpu.VMEM((2, 2, 8, 32, 512), I16),
            pltpu.VMEM((2, 2, 8, 1, 512), F32),
            pltpu.VMEM((2, 2, 8, 32, 512), I16),
            pltpu.VMEM((2, 2, 8, 1, 512), F32),
            pltpu.VMEM((8, 32, 512), F32),
            pltpu.VMEM((8, 32, 512), F32),
            pltpu.VMEM((4, 2, 32, 512), I16),
            pltpu.VMEM((4, 2, 1, 512), F32),
            pltpu.VMEM((3, 2, 32, 512), I16),
            pltpu.VMEM((3, 2, 1, 512), F32),
            pltpu.VMEM((4, 2, 32, 512), I16),
            pltpu.VMEM((4, 2, 1, 512), F32),
            pltpu.VMEM((3, 2, 32, 512), I16),
            pltpu.VMEM((3, 2, 1, 512), F32),
            pltpu.VMEM((8, 16, 512), F32),
            pltpu.VMEM((8, 16, 512), I16),
            pltpu.VMEM((8, 1, 512), F32),
            pltpu.VMEM((7, 16, 512), I16),
            pltpu.VMEM((7, 1, 512), F32),
            dma((15,)),
            dma((2,)),
            dma((2,)),
            dma((2,)),
            dma((5,)),
            dma((5,)),
            dma((2, 2, 2)),
            dma((2, 2, 2)),
            dma((4,)),
            dma((2, 4)),
            dma((2, 2)),
        ],
        compiler_params=pltpu.CompilerParams(
            collective_id=1, has_side_effects=True, vmem_limit_bytes=58 << 20
        ),
    )(*operands)


def finish_kernel(end_ref, grads_ref, end_out, grads_out, held, totals, load_sem, store_sem):
    parts = [pl.ds(i * 512, 512) for i in range(4)]
    loads = [pltpu.make_async_copy(end_ref.at[r], held.at[r], load_sem.at[i]) for i, r in enumerate(parts)]
    stores = [pltpu.make_async_copy(held.at[r], end_out.at[r], store_sem.at[i]) for i, r in enumerate(parts)]
    loads.append(pltpu.make_async_copy(grads_ref, totals, load_sem.at[4]))
    stores.append(pltpu.make_async_copy(totals, grads_out, store_sem.at[4]))
    for c in loads:
        c.start()
    for load, store in zip(loads, stores):
        load.wait()
        store.start()
    for c in stores:
        c.wait()


def finish(end, grads):
    hbm = pl.BlockSpec(memory_space=pl.ANY)
    return pl.pallas_call(
        finish_kernel,
        out_shape=[jax.ShapeDtypeStruct(end.shape, end.dtype), jax.ShapeDtypeStruct(grads.shape, grads.dtype)],
        in_specs=[hbm, hbm],
        out_specs=[hbm, hbm],
        scratch_shapes=[
            pltpu.VMEM(end.shape, end.dtype),
            pltpu.VMEM(grads.shape, grads.dtype),
            pltpu.SemaphoreType.DMA((5,)),
            pltpu.SemaphoreType.DMA((5,)),
        ],
        compiler_params=pltpu.CompilerParams(vmem_limit_bytes=58 << 20),
    )(end, grads)


def body(
    head_start,
    flow_start,
    impedance,
    friction,
    seg_count,
    junction_code,
    boundary_code,
    head_up,
    head_down,
    opening,
    window_start,
    layer_weights,
):
    row_total = window_start.shape[0] * lax.axis_size("dp") * 4
    return tuple(
        finish(
            *whole(
            8.0 / row_total,
            head_start,
            flow_start,
            impedance.T,
            friction.T,
            junction_code.T,
            seg_count[None, :],
            boundary_code[None, :],
            head_up[None, :],
            head_down[None, :],
            opening[None, :],
            window_start[None, :],
            layer_weights,
        ))
    )


def solution(mesh):
    placed = (
        P("dp", ("seg", "samp")),
        P("dp", ("seg", "samp")),
        P("dp", None),
        P("dp", None),
        P("dp"),
        P("dp", None),
        P("dp"),
        P("dp"),
        P("dp"),
        P("dp"),
        P("dp"),
        P(),
    )
    return jax.shard_map(
        body,
        mesh=mesh,
        in_specs=placed,
        out_specs=(P("dp", ("seg", "samp")), P(None, ("seg", "samp", "dp"), None)),
        check_vma=False,
    )
```
